512 devices in a mesh: dp: 4 (over y_lo, core), expert: 32 (over y_hi, z), seq: 4 (over x).
Axes of the slice: x: 4, y: 8 (y_hi: 4, y_lo: 2; y = y_hi * 2 + y_lo), z: 8, core: 2. Of those that a mesh axis runs over, the one named last changes fastest.
Arguments:
- codes: bfloat16 [65536, 2048], P(('dp', 'expert', 'seq')), may hold values from -6 to 6
- scales: float32 [65536, 16], P(('dp', 'expert', 'seq')), may hold values from 0.3 to 3
- grad_out: bfloat16 [65536, 2048], P(('dp', 'expert', 'seq')), may hold values from -6 to 6
- route_weight: float32 [65536, 2], P(('dp', 'expert', 'seq')), may hold values from 0.2 to 1
- expert_ids: int32 [65536, 2], P(('dp', 'expert', 'seq')), may hold values from 0 to 127, all different within a row; in each aligned block of 128 rows (0 to 127, 128 to 255, ...) at most 4 rows name the same one
- w_gate: bfloat16 [128, 2048, 384], P(('expert', 'seq'), 'dp'), may hold values from -0.125 to 0.125
- w_up: bfloat16 [128, 2048, 384], P(('expert', 'seq'), 'dp'), may hold values from -0.125 to 0.125
- w_down: bfloat16 [128, 384, 2048], P(('expert', 'seq'), None, 'dp'), may hold values from -0.3125 to 0.3125
Outputs:
- grad_input: bfloat16 [65536, 2048], P(('dp', 'expert', 'seq'))
- grad_gate: bfloat16 [128, 2048, 384], P(('expert', 'seq'), 'dp')
- grad_up: bfloat16 [128, 2048, 384], P(('expert', 'seq'), 'dp')
- grad_down: bfloat16 [128, 384, 2048], P(('expert', 'seq'))
The draws below stay inside these ranges and needn't reach their ends.
Inputs may be any that keep to these rules, and one draw needn't show every extreme that they name: `expert_ids`: each token names 2 different experts. Among the 128 tokens of one device no expert is named more than 4 times, and in every draw some expert is named exactly 4 times by the tokens of some device.
All inputs are finite; a program needn't handle non-finite values.
Results may differ from the reference program's by a relative error of at most 0.013.
Values may be sent and summed in bfloat16 or wider, within the bound.
No kernel may reach another device: no remote copies, remote signals or barrier semaphores. Data moves between devices by JAX's collectives and lax.ppermute only.
A program may use at most 64 MiB of HBM per device.

```python
import math
import jax
import jax.numpy as jnp
import numpy as np
from jax import lax

D = 2048
HID = 384
TOPK = 2
TOK_DEV = 128
EXPERTS = 128
CAP = 4
TOKENS = 65536
N_DP = 4
N_EXPERT = 32
N_SEQ = 4


def level_of(own_key, shape, shards, low, high):
    gain = 1.0
    for dim, parts in shards:
        draws = jax.random.uniform(jax.random.fold_in(jax.random.fold_in(own_key, 6), dim), (parts,), jnp.float32, low / len(shards), high / len(shards))
        gain = gain * jnp.repeat(jnp.exp(draws), shape[dim] // parts).reshape((-1,) + (1,) * (len(shape) - 1 - dim))
    return gain


def routed_block(rng, own, number, rows, amount, top, limit, skew):
    ranking = jax.random.permutation(rng, amount)
    packed, ordinary = load_shares(amount, rows * top, limit, skew, True), load_shares(amount, rows * top, limit, skew, False)
    places = jnp.arange(amount)

    def named(lengths, offset_by):
        used = int((lengths > 0).sum())
        fixed = max(1, used // 4)
        moved = fixed + (places - fixed + offset_by * (used - fixed)) % max(1, amount - fixed)
        return jnp.zeros((amount,), jnp.int32).at[ranking[jnp.where(places < fixed, places, moved)]].set(jnp.asarray(lengths, jnp.int32))

    lengths = jnp.where(number % 4 == 0, named(packed, number // 4), named(ordinary, number - number // 4 - 1))
    mixed = jax.random.permutation(jax.random.fold_in(own, 3), amount)
    giver, taker = mixed[0:amount // 2 * 2:2], mixed[1:amount // 2 * 2:2]
    slack = jnp.minimum(lengths[giver] - 1, limit - lengths[taker]) // 2
    slack = jnp.where((giver == ranking[0]) | (taker == ranking[0]) | (lengths[taker] == 0), 0, jnp.maximum(slack, 0))
    moved = jax.random.randint(jax.random.fold_in(own, 4), (amount // 2,), 0, 1 << 20) % (slack + 1)
    lengths = lengths.at[giver].add(-moved).at[taker].add(moved)
    items = jnp.searchsorted(jnp.cumsum(lengths), jnp.arange(rows * top), side="right").astype(jnp.int32)
    grid = items.reshape(top, rows).T
    grid = grid[jax.random.permutation(jax.random.fold_in(own, 1), rows)]
    offset_by = jax.random.randint(jax.random.fold_in(own, 2), (rows, 1), 0, top)
    return jnp.take_along_axis(grid, (jnp.arange(top)[None, :] + offset_by) % top, axis=1)


def load_shares(count, total, most, slope, full):
    portions = [(1 << 20) // math.isqrt(rank ** slope) + 1 for rank in range(1, count + 1)]
    largest = most if full else min(most, max(-(-total // count), total * portions[0] // sum(portions)))
    least = 1 if total - largest >= count - 1 else 0
    holding, surplus = [largest] + [least] * (count - 1), total - largest - least * (count - 1)
    while surplus > 0:
        movable = [i for i in range(1, count) if holding[i] < largest] or [i for i in range(1, count) if holding[i] < most]
        pool, remaining = sum([portions[i] for i in movable]), surplus
        for i in movable:
            extra = min(most - holding[i], max(1, remaining * portions[i] // pool), surplus)
            holding[i] = holding[i] + extra
            surplus = surplus - extra
    return np.array(holding)


def normal_values(rng, shape, deviation, limit, shards=(), kind=jnp.bfloat16):
    loudness = level_of(rng, shape, shards, -0.22, 0.18) if shards else 1.0
    array = jax.random.normal(rng, shape, jnp.float32) * deviation * loudness
    return jnp.minimum(jnp.maximum(array, -limit), limit).astype(kind)


def setup_inputs(seed: int = 0) -> dict:
    streams_of = jax.random.split(jax.random.key(seed), 9)
    codes = normal_values(streams_of[0], (TOKENS, D), 1.0, 6.0, ((0, 512),))
    scales = jnp.clip(jnp.exp(math.log(3.0) - 2.3025851 * jax.random.uniform(streams_of[1], (TOKENS, D // 128), jnp.float32) ** level_of(streams_of[1], (TOKENS, D // 128), ((0, 512),), -0.2, 0.2)), 0.3, 3.0)
    grad_out = normal_values(streams_of[2], (TOKENS, D), 1.0, 6.0, ((0, 512),))
    route_weight = jnp.clip(0.2 + 0.8 * jax.random.uniform(streams_of[3], (TOKENS, TOPK), jnp.float32) ** level_of(streams_of[3], (TOKENS, TOPK), ((0, 512),), -0.2, 0.2), 0.2, 1.0)
    expert_ids_keys = jax.random.split(jax.random.fold_in(streams_of[4], 1), TOKENS // TOK_DEV)
    expert_ids_turns = jax.random.permutation(jax.random.fold_in(streams_of[4], 3), TOKENS // TOK_DEV)
    expert_ids = jax.vmap(lambda own, number: routed_block(jax.random.fold_in(streams_of[4], 2), own, number, TOK_DEV, EXPERTS, TOPK, CAP, 2))(expert_ids_keys, expert_ids_turns).reshape((TOKENS, TOPK))
    w_gate = normal_values(streams_of[5], (EXPERTS, D, HID), D ** -0.5, 0.125, ((0, 128), (1, 4)))
    w_up = normal_values(streams_of[6], (EXPERTS, D, HID), D ** -0.5, 0.125, ((0, 128), (1, 4)))
    w_down = normal_values(streams_of[7], (EXPERTS, HID, D), HID ** -0.5, 0.3125, ((0, 128), (2, 4)))
    return dict(codes=codes, scales=scales, grad_out=grad_out, route_weight=route_weight, expert_ids=expert_ids, w_gate=w_gate, w_up=w_up, w_down=w_down)


def slot_table(routed, experts, capacity):
    flat = routed.reshape(-1).astype(jnp.int32)
    onehot = (flat[:, None] == jnp.arange(experts, dtype=jnp.int32)[None, :]).astype(jnp.int32)
    before = jnp.cumsum(onehot, axis=0) - onehot
    rank = jnp.sum(before * onehot, axis=1)
    return (flat * capacity + rank).astype(jnp.int32)


def expert_backward(rows_x, rows_dy, gate_mat, up_mat, down_mat):
    pre_gate = jnp.dot(rows_x, gate_mat, preferred_element_type=jnp.float32)
    pre_up = jnp.dot(rows_x, up_mat, preferred_element_type=jnp.float32)
    gate_sig = jax.nn.sigmoid(pre_gate)
    gate_act = pre_gate * gate_sig
    hidden = (gate_act * pre_up).astype(jnp.bfloat16)
    d_hidden = lax.dot_general(rows_dy, down_mat, (((1,), (1,)), ((), ())), preferred_element_type=jnp.float32)
    d_gate = (d_hidden * pre_up * gate_sig * (1.0 + pre_gate * (1.0 - gate_sig))).astype(jnp.bfloat16)
    d_up = (d_hidden * gate_act).astype(jnp.bfloat16)
    grad_d = lax.dot_general(hidden, rows_dy, (((0,), (0,)), ((), ())), preferred_element_type=jnp.float32)
    grad_g = lax.dot_general(rows_x, d_gate, (((0,), (0,)), ((), ())), preferred_element_type=jnp.float32)
    grad_u = lax.dot_general(rows_x, d_up, (((0,), (0,)), ((), ())), preferred_element_type=jnp.float32)
    back = lax.dot_general(d_gate, gate_mat, (((1,), (1,)), ((), ())), preferred_element_type=jnp.float32)
    back = back + lax.dot_general(d_up, up_mat, (((1,), (1,)), ((), ())), preferred_element_type=jnp.float32)
    return back.astype(jnp.bfloat16), grad_g, grad_u, grad_d


def group_sum(partial_value):
    rounded = lax.optimization_barrier(partial_value.astype(jnp.bfloat16))
    return jnp.sum(rounded.astype(jnp.float32), axis=0).astype(jnp.bfloat16)


def reference(codes, scales, grad_out, route_weight, expert_ids, w_gate, w_up, w_down):
    devices = N_DP * N_EXPERT * N_SEQ
    groups = N_EXPERT * N_SEQ
    assigned = TOK_DEV * TOPK
    inputs = (codes.astype(jnp.float32).reshape(TOKENS, D // 128, 128) * scales[:, :, None]).reshape(TOKENS, D).astype(jnp.bfloat16)
    scaled = (route_weight[:, :, None] * grad_out.astype(jnp.float32)[:, None, :]).astype(jnp.bfloat16)
    position = jax.vmap(lambda routed: slot_table(routed, EXPERTS, CAP))(expert_ids.reshape(devices, TOK_DEV, TOPK))
    source = jnp.arange(devices, dtype=jnp.int32)[:, None]
    x_assign = jnp.repeat(inputs.reshape(devices, TOK_DEV, D), TOPK, axis=1)
    dy_assign = scaled.reshape(devices, assigned, D)
    x_slots = jnp.zeros((devices, EXPERTS * CAP, D), jnp.bfloat16).at[source, position].set(x_assign)
    dy_slots = jnp.zeros((devices, EXPERTS * CAP, D), jnp.bfloat16).at[source, position].set(dy_assign)

    def arrange(slot_rows):
        shaped = slot_rows.reshape(N_DP, groups, EXPERTS, CAP, D)
        return jnp.moveaxis(shaped, 2, 0).reshape(EXPERTS, N_DP, groups * CAP, D)

    def per_expert(operand):
        rows_x, rows_dy, gate_mat, up_mat, down_mat = operand
        backs, grads_g, grads_u, grads_d = [], [], [], []
        for group in range(N_DP):
            back, grad_g, grad_u, grad_d = expert_backward(rows_x[group], rows_dy[group], gate_mat, up_mat, down_mat)
            backs.append(back)
            grads_g.append(grad_g)
            grads_u.append(grad_u)
            grads_d.append(grad_d)
        return (jnp.stack(backs), group_sum(jnp.stack(grads_g)), group_sum(jnp.stack(grads_u)), group_sum(jnp.stack(grads_d)))

    back_all, grad_gate, grad_up, grad_down = lax.map(per_expert, (arrange(x_slots), arrange(dy_slots), w_gate, w_up, w_down))
    back_slots = jnp.moveaxis(back_all.reshape(EXPERTS, N_DP, groups, CAP, D), 0, 2).reshape(devices, EXPERTS * CAP, D)
    picked = back_slots[source, position].reshape(devices, TOK_DEV, TOPK, D)
    grad_input = jnp.sum(picked.astype(jnp.float32), axis=2).astype(jnp.bfloat16).reshape(TOKENS, D)
    return grad_input, grad_gate, grad_up, grad_down
```

```python
import functools

import jax
import jax.numpy as jnp
from jax import lax
from jax.experimental import pallas as pl
from jax.experimental.pallas import tpu as pltpu
from jax.sharding import PartitionSpec as P

BF16 = jnp.bfloat16
F32 = jnp.float32
I32 = jnp.int32

OTHER_CORE = [(0, 1), (1, 0), (2, 3), (3, 2)]
OTHER_CHIP = [(0, 2), (2, 0), (1, 3), (3, 1)]


def iota(shape, dim):
    return lax.broadcasted_iota(I32, shape, dim)


def as_bf16(mask):
    return jnp.where(mask, 1.0, 0.0).astype(BF16)


def vmem(*_):
    return pl.BlockSpec(memory_space=pltpu.VMEM)


def send_kernel(experts, cap, dp_ref, ids_ref, weight_ref, scale_ref, codes_ref, grad_ref, send_ref, row_ref, table, place):
    step = pl.program_id(0)
    tokens, features = codes_ref.shape
    width = features // 4
    rows = send_ref.shape[0]

    @pl.when(step == 0)
    def _():
        ids = ids_ref[...]
        expert = iota((experts, tokens), 0)
        first, second = expert == ids[0:1, :], expert == ids[1:2, :]
        earlier = as_bf16(iota((tokens, tokens), 0) < iota((tokens, tokens), 1))
        count = jnp.dot(as_bf16(first | second), earlier, preferred_element_type=F32)
        rank0 = jnp.sum(jnp.where(first, count, 0.0), axis=0, keepdims=True)
        rank1 = jnp.sum(jnp.where(second, count, 0.0), axis=0, keepdims=True)
        row0 = 2 * cap * ids[0:1, :] + rank0.astype(I32)
        row1 = 2 * cap * ids[1:2, :] + rank1.astype(I32)
        place[0:1, :] = row0
        place[1:2, :] = row1
        both = jnp.concatenate([row0.astype(F32), row1.astype(F32), jnp.zeros((tokens - 2, tokens), F32)], axis=0)
        row_ref[...] = both.T.astype(I32)
        blocks = scale_ref.shape[0]
        scale = jnp.concatenate([scale_ref[...], jnp.zeros((tokens - blocks, tokens), F32)], axis=0).T
        lanes = features // blocks
        for j in range(blocks):
            part = slice(j * lanes, (j + 1) * lanes)
            table[0:tokens, part] = (codes_ref[:, part].astype(F32) * scale[:, j : j + 1]).astype(BF16)
        table[tokens : 2 * tokens, :] = grad_ref[...]

    row = iota((rows, tokens), 0) + step * rows
    is_grad = (row & cap) != 0
    base = row - (row & cap)
    in0, in1 = base == place[0:1, :], base == place[1:2, :]
    weight = jnp.sum(
        jnp.where(in0, weight_ref[0:1, :], 0.0) + jnp.where(in1, weight_ref[1:2, :], 0.0), axis=1, keepdims=True
    )
    weight = jnp.where(is_grad[:, 0:1], weight, 1.0)
    inside = in0 | in1
    pick = jnp.concatenate([as_bf16(inside & jnp.logical_not(is_grad)), as_bf16(inside & is_grad)], axis=1)
    for r in range(4):
        start = pl.multiple_of((dp_ref[0] ^ r) * width, width)
        rows_r = jnp.dot(pick, table[:, pl.ds(start, width)], preferred_element_type=F32)
        send_ref[:, r * width : (r + 1) * width] = (rows_r * weight).astype(BF16)


def rows_to_send(dp, ids, weights, scales, codes, grads, experts, cap):
    tokens, features = codes.shape
    total = 2 * experts * cap
    rows = 256
    whole = lambda a: pl.BlockSpec(a.shape, lambda i: (0, 0))
    return pl.pallas_call(
        functools.partial(send_kernel, experts, cap),
        grid=(total // rows,),
        in_specs=[pl.BlockSpec(memory_space=pltpu.SMEM)] + [whole(a) for a in (ids, weights, scales, codes, grads)],
        out_specs=[pl.BlockSpec((rows, features), lambda i: (i, 0)), pl.BlockSpec((tokens, tokens), lambda i: (0, 0))],
        out_shape=[
            jax.ShapeDtypeStruct((total, features), BF16),
            jax.ShapeDtypeStruct((tokens, tokens), I32),
        ],
        scratch_shapes=[pltpu.VMEM((2 * tokens, features), BF16), pltpu.VMEM((8, tokens), I32)],
        compiler_params=pltpu.CompilerParams(vmem_limit_bytes=32 << 20),
        cost_estimate=pl.CostEstimate(flops=2 * total * 2 * tokens * features, bytes_accessed=6 << 20, transcendentals=0),
    )(dp, ids, weights, scales, codes, grads)


def gather_matrix(cap, rows):
    q, j = iota((rows, rows), 0), iota((rows, rows), 1)
    half = rows // 2
    slot = q & (half - 1)
    row = (slot >> 2) * (2 * cap) + (slot & (cap - 1))
    return as_bf16(j == jnp.where(q >= half, row + cap, row))


def spread_matrix(cap, rows):
    q, j = iota((rows, rows), 1), iota((rows, rows), 0)
    half = rows // 2
    slot = q & (half - 1)
    row = (slot >> 2) * (2 * cap) + (slot & (cap - 1))
    return as_bf16(j == jnp.where(q >= half, row + cap, row))


def expert_kernel(cap, *refs):
    recv = refs[0]
    gate, up, down = refs[1:5], refs[5:9], refs[9:13]
    back, x_even, x_odd, dy_even, dy_odd, d_gate, d_up, hidden = refs[13:21]
    pre_g, pre_u, d_hid = refs[21:24]
    slots = d_gate.shape[0]
    width = x_even.shape[2]
    block = 256
    half = block // 2
    xs = [x_even.at[0], x_odd.at[0], x_even.at[1], x_odd.at[1]]
    dys = [dy_even.at[0], dy_odd.at[0], dy_even.at[1], dy_odd.at[1]]

    gather = gather_matrix(cap, block)
    for b in range(2 * slots // block):
        for r in range(4):
            part = jnp.dot(
                gather,
                recv[b * block : (b + 1) * block, r * width : (r + 1) * width],
                preferred_element_type=F32,
            ).astype(BF16)
            xs[r][b * half : (b + 1) * half, :] = part[:half]
            dys[r][b * half : (b + 1) * half, :] = part[half:]

    def total(rows, mats, dims):
        acc = None
        for r in range(4):
            term = lax.dot_general(rows[r][...], mats[r][...], dims, preferred_element_type=F32)
            acc = term if acc is None else acc + term
        return acc

    plain = (((1,), (0,)), ((), ()))
    turned = (((1,), (1,)), ((), ()))
    pre_g[...] = total(xs, gate, plain)
    pre_u[...] = total(xs, up, plain)
    d_hid[...] = total(dys, down, turned)

    step = 64

    @pl.loop(0, slots // step)
    def _(i):
        at = pl.ds(pl.multiple_of(i * step, step), step)
        pg, pu, dh = pre_g[at, :], pre_u[at, :], d_hid[at, :]
        sig = jax.nn.sigmoid(pg)
        act = pg * sig
        hidden[at, :] = (act * pu).astype(BF16)
        d_gate[at, :] = (dh * pu * sig * (1.0 + pg * (1.0 - sig))).astype(BF16)
        d_up[at, :] = (dh * act).astype(BF16)

    spread = spread_matrix(cap, block)
    for r in range(2):
        halves = []
        for p in range(2):
            value = lax.dot_general(d_gate[...], gate[2 * p + r][...], turned, preferred_element_type=F32)
            value = value + lax.dot_general(d_up[...], up[2 * p + r][...], turned, preferred_element_type=F32)
            halves.append(value.astype(BF16))
        for b in range(2 * slots // block):
            at = slice(b * half, (b + 1) * half)
            rows = jnp.concatenate([halves[0][at], halves[1][at]], axis=0)
            back[b * block : (b + 1) * block, r * width : (r + 1) * width] = jnp.dot(
                spread, rows, preferred_element_type=F32
            ).astype(BF16)


def expert_rows(recv, gate, up, down, cap):
    total, features = recv.shape
    slots = total // 2
    width = features // 4
    hid = gate[0].shape[1]
    shape = jax.ShapeDtypeStruct
    return pl.pallas_call(
        functools.partial(expert_kernel, cap),
        in_specs=[vmem()] * 13,
        out_specs=[vmem()] * 8,
        out_shape=[shape((total, features // 2), BF16)]
        + [shape((2, slots, width), BF16)] * 4
        + [shape((slots, hid), BF16)] * 3,
        scratch_shapes=[pltpu.VMEM((slots, hid), F32)] * 3,
        compiler_params=pltpu.CompilerParams(vmem_limit_bytes=48 << 20),
        cost_estimate=pl.CostEstimate(
            flops=2 * slots * features * hid * 5, bytes_accessed=16 << 20, transcendentals=slots * hid
        ),
    )(recv, *gate, *up, *down)


def token_kernel(cap, dp_ref, row_ref, recv_ref, out_ref):
    tokens, features = out_ref.shape
    width = features // 4
    total = recv_ref.shape[0]
    row0, row1 = row_ref[:, 0:1], row_ref[:, 1:2]
    at = iota((tokens, total), 1)
    low = as_bf16((at == row0) | (at == row1))
    high = as_bf16((at == row0 + cap) | (at == row1 + cap))
    for p, pick in enumerate((low, high)):
        for r in range(2):
            value = jnp.dot(pick, recv_ref[:, r * width : (r + 1) * width], preferred_element_type=F32)
            start = pl.multiple_of((dp_ref[0] ^ (2 * p + r)) * width, width)
            out_ref[:, pl.ds(start, width)] = value.astype(BF16)


def token_rows(dp, row_of, recv, tokens, features, cap):
    return pl.pallas_call(
        functools.partial(token_kernel, cap),
        in_specs=[pl.BlockSpec(memory_space=pltpu.SMEM), vmem(), vmem()],
        out_specs=vmem(),
        out_shape=jax.ShapeDtypeStruct((tokens, features), BF16),
        compiler_params=pltpu.CompilerParams(vmem_limit_bytes=32 << 20),
        cost_estimate=pl.CostEstimate(flops=4 * tokens * features * recv.shape[0], bytes_accessed=3 << 20, transcendentals=0),
    )(dp, row_of, recv)


def gathered(own):
    chip = lax.ppermute(own, "dp", OTHER_CHIP)
    return [own, lax.ppermute(own, "dp", OTHER_CORE), chip, lax.ppermute(chip, "dp", OTHER_CORE)]


def partial_sum(blocks, grads):
    return lax.dot_general(blocks, grads, (((1,), (0,)), ((), ())), preferred_element_type=F32).astype(BF16)


def add(a, b):
    return a.astype(F32) + b.astype(F32)


def scattered(even, odd, grads):
    given = lax.ppermute(partial_sum(odd, grads), "dp", OTHER_CORE)
    kept = add(partial_sum(even, grads), given)
    other = lax.ppermute(kept[1].astype(BF16), "dp", OTHER_CHIP)
    return add(kept[0], other).astype(BF16)


def place_kernel(dp_ref, even_ref, odd_ref, out_ref):
    width = even_ref.shape[2]
    for r, ref in enumerate((even_ref, odd_ref, even_ref, odd_ref)):
        start = pl.multiple_of((dp_ref[0] ^ r) * width, width)
        out_ref[:, pl.ds(start, width)] = ref[r // 2]


def summed(even, odd, hidden, dp):
    def product(dy):
        return jnp.stack(
            [
                lax.dot_general(hidden, dy[i], (((0,), (0,)), ((), ())), preferred_element_type=F32).astype(BF16)
                for i in range(2)
            ]
        )

    given = lax.ppermute(product(odd), "dp", OTHER_CORE)
    kept = add(product(even), given).astype(BF16)
    other = lax.ppermute(kept, "dp", OTHER_CHIP)
    mine = add(kept, other[::-1]).astype(BF16)
    theirs = lax.ppermute(mine, "dp", OTHER_CORE)
    hid, width = mine.shape[1:]
    return pl.pallas_call(
        place_kernel,
        in_specs=[pl.BlockSpec(memory_space=pltpu.SMEM), vmem(), vmem()],
        out_specs=vmem(),
        out_shape=jax.ShapeDtypeStruct((hid, 4 * width), BF16),
        compiler_params=pltpu.CompilerParams(vmem_limit_bytes=32 << 20),
        cost_estimate=pl.CostEstimate(flops=0, bytes_accessed=3 << 20, transcendentals=0),
    )(dp, mine, theirs)


def exchange(rows, groups):
    chunks = rows.reshape(groups, rows.shape[0] // groups, rows.shape[1])
    return lax.all_to_all(chunks, ("expert", "seq"), split_axis=0, concat_axis=0, tiled=True).reshape(rows.shape)


def per_device(codes, scales, grad_out, route_weight, expert_ids, w_gate, w_up, w_down):
    tokens, features = codes.shape
    groups = lax.axis_size("expert") * lax.axis_size("seq")
    cap = 2 * tokens * expert_ids.shape[1] // groups
    dp = lax.axis_index("dp").astype(I32).reshape(1)
    gate, up, down = gathered(w_gate[0]), gathered(w_up[0]), gathered(w_down[0])
    send, row_of = rows_to_send(dp, expert_ids.T, route_weight.T, scales.T, codes, grad_out, groups, cap)
    recv = exchange(send, groups)
    back, x_even, x_odd, dy_even, dy_odd, d_gate, d_up, hidden = expert_rows(recv, gate, up, down, cap)
    returned = exchange(back, groups)
    grad_gate = scattered(x_even, x_odd, d_gate)
    grad_up = scattered(x_even, x_odd, d_up)
    grad_down = summed(dy_even, dy_odd, hidden, dp)
    grad_input = token_rows(dp, row_of, returned, tokens, features, cap)
    return grad_input, grad_gate[None], grad_up[None], grad_down[None]


def solution(mesh):
    rows = P(("dp", "expert", "seq"), None)
    split = P(("expert", "seq"), "dp", None)
    return jax.shard_map(
        per_device,
        mesh=mesh,
        in_specs=(rows, rows, rows, rows, rows, split, split, P(("expert", "seq"), None, "dp")),
        out_specs=(rows, split, split, P(("expert", "seq"), None, None)),
        check_vma=False,
    )
```

```python
import functools

import jax
import jax.numpy as jnp
from jax import lax
from jax.experimental import pallas as pl
from jax.experimental.pallas import tpu as pltpu
from jax.sharding import PartitionSpec as P

BF16 = jnp.bfloat16
F32 = jnp.float32
I32 = jnp.int32
VMEM = 56 << 20
SMALL = 24 << 20
AXES = ("dp", "expert", "seq")

OTHER_CORE = [(0, 1), (1, 0), (2, 3), (3, 2)]
OTHER_CHIP = [(0, 2), (2, 0), (1, 3), (3, 1)]


def iota(shape, dim):
    return lax.broadcasted_iota(I32, shape, dim)


def as_bf16(mask):
    return jnp.where(mask, 1.0, 0.0).astype(BF16)


def dot(a, b):
    return jnp.dot(a, b, preferred_element_type=F32)


def add(a, b):
    return a.astype(F32) + b.astype(F32)


def vmem():
    return pl.BlockSpec(memory_space=pltpu.VMEM)


def smem():
    return pl.BlockSpec(memory_space=pltpu.SMEM)


def anywhere():
    return pl.BlockSpec(memory_space=pl.ANY)


def cost(flops, moved, transcendentals=0):
    return pl.CostEstimate(flops=flops, bytes_accessed=moved, transcendentals=transcendentals)


def shaped(*shape, dtype=BF16):
    return jax.ShapeDtypeStruct(shape, dtype)


def local(kernel, outs, *args, scalars=0, moved=4 << 20, flops=0):
    return pl.pallas_call(
        kernel,
        in_specs=[smem()] * scalars + [vmem()] * (len(args) - scalars),
        out_specs=[vmem()] * len(outs),
        out_shape=outs,
        compiler_params=pltpu.CompilerParams(vmem_limit_bytes=SMALL),
        cost_estimate=cost(flops, moved),
    )(*args)


def send_kernel(experts, cap, ids_ref, weight_ref, scale_ref, codes_ref, grad_ref, send_ref, row_ref, table, place):
    step = pl.program_id(0)
    tokens, features = codes_ref.shape
    rows = send_ref.shape[0]

    @pl.when(step == 0)
    def _():
        ids = ids_ref[...]
        expert = iota((experts, tokens), 0)
        first, second = expert == ids[0:1, :], expert == ids[1:2, :]
        earlier = as_bf16(iota((tokens, tokens), 0) < iota((tokens, tokens), 1))
        count = dot(as_bf16(first | second), earlier)
        rank0 = jnp.sum(jnp.where(first, count, 0.0), axis=0, keepdims=True)
        rank1 = jnp.sum(jnp.where(second, count, 0.0), axis=0, keepdims=True)
        row0 = 2 * cap * ids[0:1, :] + rank0.astype(I32)
        row1 = 2 * cap * ids[1:2, :] + rank1.astype(I32)
        place[0:1, :] = row0
        place[1:2, :] = row1
        both = jnp.concatenate([row0.astype(F32), row1.astype(F32), jnp.zeros((tokens - 2, tokens), F32)], axis=0)
        row_ref[...] = both.T.astype(I32)
        blocks = scale_ref.shape[0]
        scale = jnp.concatenate([scale_ref[...], jnp.zeros((tokens - blocks, tokens), F32)], axis=0).T
        lanes = features // blocks
        for j in range(blocks):
            part = slice(j * lanes, (j + 1) * lanes)
            table[0:tokens, part] = (codes_ref[:, part].astype(F32) * scale[:, j : j + 1]).astype(BF16)
        table[tokens : 2 * tokens, :] = grad_ref[...]

    row = iota((rows, tokens), 0) + step * rows
    is_grad = (row & cap) != 0
    base = row - (row & cap)
    in0, in1 = base == place[0:1, :], base == place[1:2, :]
    weight = jnp.sum(
        jnp.where(in0, weight_ref[0:1, :], 0.0) + jnp.where(in1, weight_ref[1:2, :], 0.0), axis=1, keepdims=True
    )
    weight = jnp.where(is_grad[:, 0:1], weight, 1.0)
    inside = in0 | in1
    pick = jnp.concatenate([as_bf16(inside & jnp.logical_not(is_grad)), as_bf16(inside & is_grad)], axis=1)
    width = 512
    for start in range(0, features, width):
        part = slice(start, start + width)
        send_ref[:, part] = (dot(pick, table[:, part]) * weight).astype(BF16)


def rows_to_send(ids, weights, scales, codes, grads, experts, cap):
    tokens, features = codes.shape
    total = 2 * experts * cap
    rows = 256
    whole = lambda a: pl.BlockSpec(a.shape, lambda i: (0, 0))
    return pl.pallas_call(
        functools.partial(send_kernel, experts, cap),
        grid=(total // rows,),
        in_specs=[whole(a) for a in (ids, weights, scales, codes, grads)],
        out_specs=[pl.BlockSpec((rows, features), lambda i: (i, 0)), pl.BlockSpec((tokens, tokens), lambda i: (0, 0))],
        out_shape=[shaped(total, features), shaped(tokens, tokens, dtype=I32)],
        scratch_shapes=[pltpu.VMEM((2 * tokens, features), BF16), pltpu.VMEM((8, tokens), I32)],
        compiler_params=pltpu.CompilerParams(vmem_limit_bytes=VMEM),
        cost_estimate=cost(1 << 38, 6 << 20),
    )(ids, weights, scales, codes, grads)


def pack_kernel(gate, up, down, out):
    out[0] = gate[...]
    out[1] = up[...]
    out[2] = down[...].T


def merge_kernel(own, chip, out):
    out[0] = own[...]
    out[1] = chip[...]


def arrange_kernel(dp_ref, mine, theirs, pre_mat, down_mat, back_mat):
    width, hid = mine.shape[2:]
    for r, ref in enumerate((mine, theirs, mine, theirs)):
        at = pl.ds(pl.multiple_of((dp_ref[0] ^ r) * width, width), width)
        for k in range(2):
            value = ref[r // 2, k]
            pre_mat[at, k * hid : (k + 1) * hid] = value
            back_mat[k * hid : (k + 1) * hid, at] = value.T
        down_mat[at, :] = ref[r // 2, 2]


def expert_weights(gate, up, down, dp):
    width, hid = gate.shape
    (own,) = local(pack_kernel, [shaped(3, width, hid)], gate, up, down)
    chip = lax.ppermute(own, "dp", OTHER_CHIP)
    (mine,) = local(merge_kernel, [shaped(2, 3, width, hid)], own, chip, flops=1 << 38)
    theirs = lax.ppermute(mine, "dp", OTHER_CORE)
    full = 4 * width
    return local(
        arrange_kernel,
        [shaped(full, 2 * hid), shaped(full, hid), shaped(2 * hid, full)],
        dp,
        mine,
        theirs,
        scalars=1,
        moved=12 << 20,
    )


def chunk_row(cap, rows, index):
    half = rows // 2
    slot = index & (half - 1)
    row = (slot // cap) * (2 * cap) + (slot & (cap - 1))
    return jnp.where(index >= half, row + cap, row)


def gather_matrix(cap, rows):
    return as_bf16(iota((rows, rows), 1) == chunk_row(cap, rows, iota((rows, rows), 0)))


def spread_matrix(cap, rows):
    return as_bf16(iota((rows, rows), 0) == chunk_row(cap, rows, iota((rows, rows), 1)))


def expert_kernel(
    cap, recv, pre_mat, down_mat, back_mat, back, x_out, dy_out, d_gu, hidden, landed, x, dy, pre, d_hid, dx, recv_sem, out_sem
):
    slots, features = x.shape
    hid = hidden.shape[1]
    blocks, block = landed.shape[:2]
    half = block // 2
    width = 512

    arrivals = [
        pltpu.make_async_copy(recv.at[pl.ds(b * block, block)], landed.at[b], recv_sem.at[b]) for b in range(blocks)
    ]
    for copy in arrivals:
        copy.start()
    gather = gather_matrix(cap, block)
    for b in range(blocks):
        arrivals[b].wait()
        at = slice(b * half, (b + 1) * half)
        for start in range(0, features, width):
            part = slice(start, start + width)
            rows = dot(gather, landed[b, :, part]).astype(BF16)
            x[at, part] = rows[:half]
            dy[at, part] = rows[half:]
    departures = [pltpu.make_async_copy(x, x_out, out_sem.at[0]), pltpu.make_async_copy(dy, dy_out, out_sem.at[1])]
    for copy in departures:
        copy.start()

    pre[...] = dot(x[...], pre_mat[...])
    d_hid[...] = dot(dy[...], down_mat[...])

    step = 64

    @pl.loop(0, slots // step)
    def _(i):
        at = pl.ds(pl.multiple_of(i * step, step), step)
        pg, pu, dh = pre[at, 0:hid], pre[at, hid : 2 * hid], d_hid[at, :]
        sig = jax.nn.sigmoid(pg)
        act = pg * sig
        hidden[at, :] = (act * pu).astype(BF16)
        d_gu[at, 0:hid] = (dh * pu * sig * (1.0 + pg * (1.0 - sig))).astype(BF16)
        d_gu[at, hid : 2 * hid] = (dh * act).astype(BF16)

    for start in range(0, features, width):
        part = slice(start, start + width)
        dx[:, part] = dot(d_gu[...], back_mat[:, part]).astype(BF16)
    spread = spread_matrix(cap, block)
    for b in range(blocks):
        at = slice(b * half, (b + 1) * half)
        for start in range(0, features // 2, width):
            low, high = slice(start, start + width), slice(features // 2 + start, features // 2 + start + width)
            rows = jnp.concatenate([dx[at, low], dx[at, high]], axis=0)
            back[b * block : (b + 1) * block, low] = dot(spread, rows).astype(BF16)
    for copy in departures:
        copy.wait()


def expert_rows(recv, pre_mat, down_mat, back_mat, cap):
    total, features = recv.shape
    slots = total // 2
    hid = down_mat.shape[1]
    block = 256
    return pl.pallas_call(
        functools.partial(expert_kernel, cap),
        in_specs=[anywhere()] + [vmem()] * 3,
        out_specs=[vmem()] + [anywhere()] * 2 + [vmem()] * 2,
        out_shape=[
            shaped(total, features // 2),
            shaped(slots, features),
            shaped(slots, features),
            shaped(slots, 2 * hid),
            shaped(slots, hid),
        ],
        scratch_shapes=[
            pltpu.VMEM((total // block, block, features), BF16),
            pltpu.VMEM((slots, features), BF16),
            pltpu.VMEM((slots, features), BF16),
            pltpu.VMEM((slots, 2 * hid), F32),
            pltpu.VMEM((slots, hid), F32),
            pltpu.VMEM((slots, features), BF16),
            pltpu.SemaphoreType.DMA((total // block,)),
            pltpu.SemaphoreType.DMA((2,)),
        ],
        compiler_params=pltpu.CompilerParams(vmem_limit_bytes=VMEM),
        cost_estimate=cost(2 * slots * features * hid * 5, 16 << 20, slots * hid),
    )(recv, pre_mat, down_mat, back_mat)


def odd_kernel(dp_ref, x, dy, d_gu, hidden, out, turned_out, turned):
    @pl.when(pl.program_id(0) == 0)
    def _():
        wide = d_gu.shape[1]
        turned[0:wide, :] = d_gu[...].T
        turned[wide:, :] = hidden[...].T
        turned_out[...] = turned[...]

    even_kernel(dp_ref, x, dy, turned, out)


def even_kernel(dp_ref, x, dy, turned, out):
    hid = out.shape[1]
    for k, rows in enumerate((x, x, dy)):
        out[k] = dot(turned[k * hid : (k + 1) * hid, :], rows[...]).astype(BF16)


def partial_grads(kernel, first, dp, x, dy, grads, outs, scratch):
    slots, features = x.shape
    width = features // 4
    rows = pl.BlockSpec((slots, width), lambda i, dp: (0, dp[0] ^ (2 * i + first)))
    whole = lambda a: pl.BlockSpec(a.shape, lambda i, dp: (0, 0))
    hid = outs[0].shape[2]
    return pl.pallas_call(
        kernel,
        grid_spec=pltpu.PrefetchScalarGridSpec(
            num_scalar_prefetch=1,
            grid=(2,),
            in_specs=[rows, rows] + [whole(g) for g in grads],
            out_specs=[pl.BlockSpec((None, 3, hid, width), lambda i, dp: (i, 0, 0, 0))] + [whole(o) for o in outs[1:]],
            scratch_shapes=scratch,
        ),
        out_shape=outs,
        compiler_params=pltpu.CompilerParams(vmem_limit_bytes=VMEM),
        cost_estimate=cost(12 * slots * width * hid, 6 << 20),
    )(dp, x, dy, *grads)


def first_kernel(even, given, down, gate_up, keep):
    for r in range(2):
        down[r] = add(even[r, 2], given[r, 2]).astype(BF16)
    for k in range(2):
        gate_up[k] = add(even[1, k], given[1, k]).astype(BF16)
        keep[k] = add(even[0, k], given[0, k]).astype(BF16)


def down_kernel(sent, other, out):
    out[0] = add(sent[0], other[1]).astype(BF16)
    out[1] = add(sent[1], other[0]).astype(BF16)


def gate_up_kernel(keep, other, gate, up):
    gate[...] = add(keep[0], other[0]).astype(BF16).T
    up[...] = add(keep[1], other[1]).astype(BF16).T


def place_kernel(dp_ref, even, odd, out):
    width = even.shape[2]
    for r, ref in enumerate((even, odd, even, odd)):
        out[:, pl.ds(pl.multiple_of((dp_ref[0] ^ r) * width, width), width)] = ref[r // 2]


def summed_grads(x, dy, d_gu, hidden, dp):
    slots, features = x.shape
    width, hid = features // 4, hidden.shape[1]
    part = shaped(2, 3, hid, width)
    turned = shaped(3 * hid, slots)
    odd, grads = partial_grads(
        odd_kernel, 1, dp, x, dy, (d_gu, hidden), [part, turned], [pltpu.VMEM(turned.shape, BF16)]
    )
    given = lax.ppermute(odd, "dp", OTHER_CORE)
    (even,) = partial_grads(even_kernel, 0, dp, x, dy, (grads,), [part], [])
    two = shaped(2, hid, width)
    down, gate_up, keep = local(first_kernel, [two] * 3, even, given)
    down_other = lax.ppermute(down, "dp", OTHER_CHIP)
    gate_up_other = lax.ppermute(gate_up, "dp", OTHER_CHIP)
    (mine,) = local(down_kernel, [two], down, down_other)
    theirs = lax.ppermute(mine, "dp", OTHER_CORE)
    (grad_down,) = local(place_kernel, [shaped(hid, features)], dp, mine, theirs, scalars=1)
    grad_gate, grad_up = local(gate_up_kernel, [shaped(width, hid)] * 2, keep, gate_up_other)
    return grad_gate, grad_up, grad_down


def token_kernel(cap, row_ref, recv_ref, out_ref):
    tokens, features = out_ref.shape
    total, half = recv_ref.shape
    row0, row1 = row_ref[:, 0:1], row_ref[:, 1:2]
    at = iota((tokens, total), 1)
    low = as_bf16((at == row0) | (at == row1))
    high = as_bf16((at == row0 + cap) | (at == row1 + cap))
    width = 512
    for p, pick in enumerate((low, high)):
        for start in range(0, half, width):
            value = dot(pick, recv_ref[:, start : start + width])
            out_ref[:, p * half + start : p * half + start + width] = value.astype(BF16)


def token_rows(row_of, recv, tokens, features, cap):
    return pl.pallas_call(
        functools.partial(token_kernel, cap),
        in_specs=[vmem(), vmem()],
        out_specs=vmem(),
        out_shape=shaped(tokens, features),
        compiler_params=pltpu.CompilerParams(vmem_limit_bytes=SMALL),
        cost_estimate=cost(4 * tokens * features * recv.shape[0], 3 << 20),
    )(row_of, recv)


def exchange(rows, experts):
    near = experts // 2
    members = [
        [(2 * (chip ^ (e // near)) + core) * experts + e for e in range(experts)] for chip in range(2) for core in range(2)
    ]
    chunks = rows.reshape(experts, rows.shape[0] // experts, rows.shape[1])
    moved = lax.all_to_all(chunks, AXES, split_axis=0, concat_axis=0, axis_index_groups=members, tiled=True)
    return moved.reshape(rows.shape)


def per_device(codes, scales, grad_out, route_weight, expert_ids, w_gate, w_up, w_down):
    tokens, features = codes.shape
    experts = lax.axis_size("expert") * lax.axis_size("seq")
    cap = 2 * tokens * expert_ids.shape[1] // experts
    dp = lax.axis_index("dp").astype(I32).reshape(1)
    mats = expert_weights(w_gate[0], w_up[0], w_down[0], dp)
    send, row_of = rows_to_send(expert_ids.T, route_weight.T, scales.T, codes, grad_out, experts, cap)
    recv = exchange(send, experts)
    back, x, dy, d_gu, hidden = expert_rows(recv, *mats, cap)
    returned = exchange(back, experts)
    grad_gate, grad_up, grad_down = summed_grads(x, dy, d_gu, hidden, dp)
    grad_input = token_rows(row_of, returned, tokens, features, cap)
    return grad_input, grad_gate[None], grad_up[None], grad_down[None]


def solution(mesh):
    rows = P(AXES, None)
    split = P(("expert", "seq"), "dp", None)
    return jax.shard_map(
        per_device,
        mesh=mesh,
        in_specs=(rows, rows, rows, rows, rows, split, split, P(("expert", "seq"), None, "dp")),
        out_specs=(rows, split, split, P(("expert", "seq"), None, None)),
        check_vma=False,
    )
```

```python
import functools

import jax
import jax.numpy as jnp
from jax import lax
from jax.experimental import pallas as pl
from jax.experimental.pallas import tpu as pltpu
from jax.sharding import PartitionSpec as P

BF16 = jnp.bfloat16
F32 = jnp.float32
I32 = jnp.int32
VMEM = 56 << 20
SMALL = 24 << 20
AXES = ("dp", "expert", "seq")

OTHER_CORE = [(0, 1), (1, 0), (2, 3), (3, 2)]
OTHER_CHIP = [(0, 2), (2, 0), (1, 3), (3, 1)]


def iota(shape, dim):
    return lax.broadcasted_iota(I32, shape, dim)


def as_bf16(mask):
    return jnp.where(mask, 1.0, 0.0).astype(BF16)


def dot(a, b):
    return jnp.dot(a, b, preferred_element_type=F32)


def dot_turned(a, b):
    return lax.dot_general(a, b, (((1,), (1,)), ((), ())), preferred_element_type=F32)


def add(a, b):
    return a.astype(F32) + b.astype(F32)


def vmem():
    return pl.BlockSpec(memory_space=pltpu.VMEM)


def smem():
    return pl.BlockSpec(memory_space=pltpu.SMEM)


def anywhere():
    return pl.BlockSpec(memory_space=pl.ANY)


def cost(flops, moved, transcendentals=0):
    return pl.CostEstimate(flops=flops, bytes_accessed=moved, transcendentals=transcendentals)


def shaped(*shape, dtype=BF16):
    return jax.ShapeDtypeStruct(shape, dtype)


def local(kernel, outs, *args, scalars=0, moved=4 << 20, flops=0, limit=SMALL):
    return pl.pallas_call(
        kernel,
        in_specs=[smem()] * scalars + [vmem()] * (len(args) - scalars),
        out_specs=[vmem()] * len(outs),
        out_shape=outs,
        compiler_params=pltpu.CompilerParams(vmem_limit_bytes=limit),
        cost_estimate=cost(flops, moved),
    )(*args)


ORDER = (4, 6, 0, 3, 5, 2, 1)


def chunk_of(expert):
    return sum(((expert >> bit) & 1) << k for k, bit in enumerate(ORDER))


def send_kernel(experts, cap, ids_ref, weight_ref, scale_ref, codes_ref, grad_ref, send_ref, row_ref, table, place):
    step = pl.program_id(0)
    tokens, features = codes_ref.shape
    rows = send_ref.shape[0]

    @pl.when(step == 0)
    def _():
        ids = ids_ref[...]
        expert = iota((experts, tokens), 0)
        first, second = expert == ids[0:1, :], expert == ids[1:2, :]
        earlier = as_bf16(iota((tokens, tokens), 0) < iota((tokens, tokens), 1))
        count = dot(as_bf16(first | second), earlier)
        rank0 = jnp.sum(jnp.where(first, count, 0.0), axis=0, keepdims=True)
        rank1 = jnp.sum(jnp.where(second, count, 0.0), axis=0, keepdims=True)
        row0 = 2 * cap * chunk_of(ids[0:1, :]) + rank0.astype(I32)
        row1 = 2 * cap * chunk_of(ids[1:2, :]) + rank1.astype(I32)
        place[0:1, :] = row0
        place[1:2, :] = row1
        both = jnp.concatenate([row0.astype(F32), row1.astype(F32), jnp.zeros((tokens - 2, tokens), F32)], axis=0)
        row_ref[...] = both.T.astype(I32)
        blocks = scale_ref.shape[0]
        scale = jnp.concatenate([scale_ref[...], jnp.zeros((tokens - blocks, tokens), F32)], axis=0).T
        lanes = features // blocks
        for j in range(blocks):
            part = slice(j * lanes, (j + 1) * lanes)
            table[0:tokens, part] = (codes_ref[:, part].astype(F32) * scale[:, j : j + 1]).astype(BF16)
        table[tokens : 2 * tokens, :] = grad_ref[...]

    row = iota((rows, tokens), 0) + step * rows
    is_grad = (row & cap) != 0
    base = row - (row & cap)
    in0, in1 = base == place[0:1, :], base == place[1:2, :]
    weight = jnp.sum(
        jnp.where(in0, weight_ref[0:1, :], 0.0) + jnp.where(in1, weight_ref[1:2, :], 0.0), axis=1, keepdims=True
    )
    weight = jnp.where(is_grad[:, 0:1], weight, 1.0)
    inside = in0 | in1
    pick = jnp.concatenate([as_bf16(inside & jnp.logical_not(is_grad)), as_bf16(inside & is_grad)], axis=1)
    width = 512
    for start in range(0, features, width):
        part = slice(start, start + width)
        send_ref[:, part] = (dot(pick, table[:, part]) * weight).astype(BF16)


def rows_to_send(ids, weights, scales, codes, grads, experts, cap):
    tokens, features = codes.shape
    total = 2 * experts * cap
    rows = 256
    whole = lambda a: pl.BlockSpec(a.shape, lambda i: (0, 0))
    return pl.pallas_call(
        functools.partial(send_kernel, experts, cap),
        grid=(total // rows,),
        in_specs=[whole(a) for a in (ids, weights, scales, codes, grads)],
        out_specs=[pl.BlockSpec((rows, features), lambda i: (i, 0)), pl.BlockSpec((tokens, tokens), lambda i: (0, 0))],
        out_shape=[shaped(total, features), shaped(tokens, tokens, dtype=I32)],
        scratch_shapes=[pltpu.VMEM((2 * tokens, features), BF16), pltpu.VMEM((8, tokens), I32)],
        compiler_params=pltpu.CompilerParams(vmem_limit_bytes=VMEM),
        cost_estimate=cost(1 << 38, 6 << 20),
    )(ids, weights, scales, codes, grads)


def pack_kernel(gate, up, down, out):
    out[0] = gate[...]
    out[1] = up[...]
    out[2] = down[...].T


def merge_kernel(own, chip, out):
    out[0] = own[...]
    out[1] = chip[...]


def arrange_kernel(dp_ref, mine, theirs, pre_mat, down_mat):
    width, hid = mine.shape[2:]
    for r, ref in enumerate((mine, theirs, mine, theirs)):
        at = pl.ds(pl.multiple_of((dp_ref[0] ^ r) * width, width), width)
        for k in range(2):
            pre_mat[at, k * hid : (k + 1) * hid] = ref[r // 2, k]
        down_mat[at, :] = ref[r // 2, 2]


def expert_weights(gate, up, down, dp):
    width, hid = gate.shape
    (own,) = local(pack_kernel, [shaped(3, width, hid)], gate, up, down, limit=VMEM)
    chip = lax.ppermute(own, "dp", OTHER_CHIP)
    (mine,) = local(merge_kernel, [shaped(2, 3, width, hid)], own, chip, flops=1 << 38)
    theirs = lax.ppermute(mine, "dp", OTHER_CORE)
    full = 4 * width
    return local(
        arrange_kernel,
        [shaped(full, 2 * hid), shaped(full, hid)],
        dp,
        mine,
        theirs,
        scalars=1,
        moved=12 << 20,
    )


def chunk_row(cap, rows, index):
    half = rows // 2
    slot = index & (half - 1)
    row = (slot // cap) * (2 * cap) + (slot & (cap - 1))
    return jnp.where(index >= half, row + cap, row)


def gather_matrix(cap, rows):
    return as_bf16(iota((rows, rows), 1) == chunk_row(cap, rows, iota((rows, rows), 0)))


def spread_matrix(cap, rows):
    return as_bf16(iota((rows, rows), 0) == chunk_row(cap, rows, iota((rows, rows), 1)))


def expert_kernel(
    cap,
    recv, pre_hbm, down_hbm,
    back_out, d_gu_out, hidden_out,
    landed, pre_mat, down_mat, x, dy, pre, d_hid, d_gu, hidden, dx, back,
    recv_sem, mat_sem, out_sem, back_sem,
):
    slots, features = x.shape
    hid = hidden.shape[1]
    blocks, block = landed.shape[:2]
    half = block // 2
    width = 512

    arrivals = [
        pltpu.make_async_copy(recv.at[pl.ds(b * block, block)], landed.at[b], recv_sem.at[b]) for b in range(blocks)
    ]
    mats = [
        pltpu.make_async_copy(src, dst, mat_sem.at[k])
        for k, (src, dst) in enumerate(((pre_hbm, pre_mat), (down_hbm, down_mat)))
    ]
    leaving = [
        pltpu.make_async_copy(src, dst, out_sem.at[k])
        for k, (src, dst) in enumerate(((d_gu, d_gu_out), (hidden, hidden_out)))
    ]
    returning = [
        pltpu.make_async_copy(back.at[b], back_out.at[pl.ds(b * block, block)], back_sem.at[b]) for b in range(blocks)
    ]
    for copy in arrivals + mats:
        copy.start()
    gather = gather_matrix(cap, block)
    for b in range(blocks):
        arrivals[b].wait()
        at = slice(b * half, (b + 1) * half)
        for start in range(0, features, width):
            part = slice(start, start + width)
            rows = dot(gather, landed[b, :, part]).astype(BF16)
            x[at, part] = rows[:half]
            dy[at, part] = rows[half:]
    mats[0].wait()
    wide = 256
    for m in range(0, slots, wide):
        pre[m : m + wide] = dot(x[m : m + wide], pre_mat[...])
    mats[1].wait()
    d_hid[...] = dot(dy[...], down_mat[...])

    step = 64

    @pl.loop(0, slots // step)
    def _(i):
        at = pl.ds(pl.multiple_of(i * step, step), step)
        pg, pu, dh = pre[at, 0:hid], pre[at, hid : 2 * hid], d_hid[at, :]
        sig = jax.nn.sigmoid(pg)
        act = pg * sig
        hidden[at, :] = (act * pu).astype(BF16)
        d_gu[at, 0:hid] = (dh * pu * sig * (1.0 + pg * (1.0 - sig))).astype(BF16)
        d_gu[at, hid : 2 * hid] = (dh * act).astype(BF16)

    for copy in leaving:
        copy.start()
    for start in range(0, features, width):
        part = slice(start, start + width)
        dx[:, part] = dot_turned(d_gu[...], pre_mat[part, :]).astype(BF16)
    spread = spread_matrix(cap, block)
    for b in range(blocks):
        at = slice(b * half, (b + 1) * half)
        for start in range(0, features // 2, width):
            low, high = slice(start, start + width), slice(features // 2 + start, features // 2 + start + width)
            rows = jnp.concatenate([dx[at, low], dx[at, high]], axis=0)
            back[b, :, low] = dot(spread, rows).astype(BF16)
        returning[b].start()
    for copy in leaving + returning:
        copy.wait()


def expert_rows(recv, pre_mat, down_mat, cap):
    total, features = recv.shape
    slots = total // 2
    hid = down_mat.shape[1]
    block = 256
    blocks = total // block
    outs = [(total, features // 2), (slots, 2 * hid), (slots, hid)]
    dma = pltpu.SemaphoreType.DMA
    return pl.pallas_call(
        functools.partial(expert_kernel, cap),
        in_specs=[anywhere()] * 3,
        out_specs=[anywhere()] * 3,
        out_shape=[shaped(*shape) for shape in outs],
        scratch_shapes=[
            pltpu.VMEM((blocks, block, features), BF16),
            pltpu.VMEM(pre_mat.shape, BF16),
            pltpu.VMEM(down_mat.shape, BF16),
            pltpu.VMEM((slots, features), BF16),
            pltpu.VMEM((slots, features), BF16),
            pltpu.VMEM((slots, 2 * hid), F32),
            pltpu.VMEM((slots, hid), F32),
            pltpu.VMEM((slots, 2 * hid), BF16),
            pltpu.VMEM((slots, hid), BF16),
            pltpu.VMEM((slots, features), BF16),
            pltpu.VMEM((blocks, block, features // 2), BF16),
            dma((blocks,)),
            dma((2,)),
            dma((2,)),
            dma((blocks,)),
        ],
        compiler_params=pltpu.CompilerParams(vmem_limit_bytes=VMEM),
        cost_estimate=cost(2 * slots * features * hid * 5, 16 << 20, slots * hid),
    )(recv, pre_mat, down_mat)


def odd_kernel(cap, dp_ref, recv, d_gu, hidden, out, turned_out, turned, x, dy):
    @pl.when(pl.program_id(0) == 0)
    def _():
        wide = d_gu.shape[1]
        turned[0:wide, :] = d_gu[...].T
        turned[wide:, :] = hidden[...].T
        turned_out[...] = turned[...]

    even_kernel(cap, dp_ref, recv, turned, out, x, dy)


def even_kernel(cap, dp_ref, recv, turned, out, x, dy):
    hid = out.shape[1]
    block = 256
    half = block // 2
    gather = gather_matrix(cap, block)
    for b in range(recv.shape[0] // block):
        rows = dot(gather, recv[b * block : (b + 1) * block, :]).astype(BF16)
        at = slice(b * half, (b + 1) * half)
        x[at, :] = rows[:half]
        dy[at, :] = rows[half:]
    for k, rows in enumerate((x, x, dy)):
        out[k] = dot(turned[k * hid : (k + 1) * hid, :], rows[...]).astype(BF16)


def partial_grads(kernel, first, dp, recv, grads, outs, scratch, cap):
    total, features = recv.shape
    width = features // 4
    whole = lambda a: pl.BlockSpec(a.shape, lambda i, dp: (0, 0))
    hid = outs[0].shape[2]
    return pl.pallas_call(
        functools.partial(kernel, cap),
        grid_spec=pltpu.PrefetchScalarGridSpec(
            num_scalar_prefetch=1,
            grid=(2,),
            in_specs=[pl.BlockSpec((total, width), lambda i, dp: (0, dp[0] ^ (2 * i + first)))] + [whole(g) for g in grads],
            out_specs=[pl.BlockSpec((None, 3, hid, width), lambda i, dp: (i, 0, 0, 0))] + [whole(o) for o in outs[1:]],
            scratch_shapes=scratch + [pltpu.VMEM((total // 2, width), BF16)] * 2,
        ),
        out_shape=outs,
        compiler_params=pltpu.CompilerParams(vmem_limit_bytes=VMEM),
        cost_estimate=cost(6 * total * width * hid, 6 << 20),
    )(dp, recv, *grads)


def first_kernel(even, given, down, gate_up, keep):
    for r in range(2):
        down[r] = add(even[r, 2], given[r, 2]).astype(BF16)
    for k in range(2):
        gate_up[k] = add(even[1, k], given[1, k]).astype(BF16)
        keep[k] = add(even[0, k], given[0, k]).astype(BF16)


def down_kernel(sent, other, out):
    out[0] = add(sent[0], other[1]).astype(BF16)
    out[1] = add(sent[1], other[0]).astype(BF16)


def gate_up_kernel(keep, other, gate, up):
    gate[...] = add(keep[0], other[0]).astype(BF16).T
    up[...] = add(keep[1], other[1]).astype(BF16).T


def place_kernel(dp_ref, even, odd, out):
    width = even.shape[2]
    for r, ref in enumerate((even, odd, even, odd)):
        out[:, pl.ds(pl.multiple_of((dp_ref[0] ^ r) * width, width), width)] = ref[r // 2]


def summed_grads(recv, d_gu, hidden, dp, grad_input, cap):
    features = recv.shape[1]
    slots, hid = hidden.shape
    width = features // 4
    part = shaped(2, 3, hid, width)
    turned = shaped(3 * hid, slots)
    odd, grads = partial_grads(
        odd_kernel, 1, dp, recv, (d_gu, hidden), [part, turned], [pltpu.VMEM(turned.shape, BF16)], cap
    )
    given = lax.ppermute(odd, "dp", OTHER_CORE)
    (even,) = partial_grads(even_kernel, 0, dp, recv, (grads,), [part], [], cap)
    two = shaped(2, hid, width)
    down, gate_up, keep = local(first_kernel, [two] * 3, even, given)
    down_other = lax.ppermute(down, "dp", OTHER_CHIP)
    gate_up_other = lax.ppermute(gate_up, "dp", OTHER_CHIP)
    (mine,) = local(down_kernel, [two], down, down_other)
    theirs = lax.ppermute(mine, "dp", OTHER_CORE)
    (grad_down,) = local(place_kernel, [shaped(hid, features)], dp, mine, theirs, scalars=1)
    grad_gate, grad_up = local(gate_up_kernel, [shaped(width, hid)] * 2, keep, gate_up_other)
    return grad_input, grad_gate, grad_up, grad_down


def token_kernel(cap, row_ref, recv_ref, out_ref):
    tokens, features = out_ref.shape
    total, half = recv_ref.shape
    row0, row1 = row_ref[:, 0:1], row_ref[:, 1:2]
    at = iota((tokens, total), 1)
    low = as_bf16((at == row0) | (at == row1))
    high = as_bf16((at == row0 + cap) | (at == row1 + cap))
    width = 512
    for p, pick in enumerate((low, high)):
        for start in range(0, half, width):
            value = dot(pick, recv_ref[:, start : start + width])
            out_ref[:, p * half + start : p * half + start + width] = value.astype(BF16)


def token_rows(row_of, recv, tokens, features, cap):
    return pl.pallas_call(
        functools.partial(token_kernel, cap),
        in_specs=[vmem(), vmem()],
        out_specs=vmem(),
        out_shape=shaped(tokens, features),
        compiler_params=pltpu.CompilerParams(vmem_limit_bytes=SMALL),
        cost_estimate=cost(4 * tokens * features * recv.shape[0], 3 << 20),
    )(row_of, recv)


def exchange(rows, experts):
    near = experts // 2
    order = sorted(range(experts), key=chunk_of)
    members = [
        [(2 * (chip ^ (e // near)) + core) * experts + e for e in order] for chip in range(2) for core in range(2)
    ]
    chunks = rows.reshape(experts, rows.shape[0] // experts, rows.shape[1])
    moved = lax.all_to_all(chunks, AXES, split_axis=0, concat_axis=0, axis_index_groups=members, tiled=True)
    return moved.reshape(rows.shape)


def per_device(codes, scales, grad_out, route_weight, expert_ids, w_gate, w_up, w_down):
    tokens, features = codes.shape
    experts = lax.axis_size("expert") * lax.axis_size("seq")
    cap = 2 * tokens * expert_ids.shape[1] // experts
    dp = lax.axis_index("dp").astype(I32).reshape(1)
    mats = expert_weights(w_gate[0], w_up[0], w_down[0], dp)
    send, row_of = rows_to_send(expert_ids.T, route_weight.T, scales.T, codes, grad_out, experts, cap)
    recv = exchange(send, experts)
    back, d_gu, hidden = expert_rows(recv, *mats, cap)
    returned = exchange(back, experts)
    grad_input = token_rows(row_of, returned, tokens, features, cap)
    grad_input, grad_gate, grad_up, grad_down = summed_grads(recv, d_gu, hidden, dp, grad_input, cap)
    return grad_input, grad_gate[None], grad_up[None], grad_down[None]


def solution(mesh):
    rows = P(AXES, None)
    split = P(("expert", "seq"), "dp", None)
    return jax.shard_map(
        per_device,
        mesh=mesh,
        in_specs=(rows, rows, rows, rows, rows, split, split, P(("expert", "seq"), None, "dp")),
        out_specs=(rows, split, split, P(("expert", "seq"), None, None)),
        check_vma=False,
    )
```

```python
import functools

import jax
import jax.numpy as jnp
from jax import lax
from jax.experimental import pallas as pl
from jax.experimental.pallas import tpu as pltpu
from jax.sharding import PartitionSpec as P

BF16 = jnp.bfloat16
F32 = jnp.float32
I32 = jnp.int32
VMEM = 56 << 20
SMALL = 24 << 20
AXES = ("dp", "expert", "seq")

OTHER_CORE = [(0, 1), (1, 0), (2, 3), (3, 2)]
OTHER_CHIP = [(0, 2), (2, 0), (1, 3), (3, 1)]


def iota(shape, dim):
    return lax.broadcasted_iota(I32, shape, dim)


def as_bf16(mask):
    return jnp.where(mask, 1.0, 0.0).astype(BF16)


def dot(a, b):
    return jnp.dot(a, b, preferred_element_type=F32)


def dot_turned(a, b):
    return lax.dot_general(a, b, (((1,), (1,)), ((), ())), preferred_element_type=F32)


def add(a, b):
    return a.astype(F32) + b.astype(F32)


def vmem():
    return pl.BlockSpec(memory_space=pltpu.VMEM)


def smem():
    return pl.BlockSpec(memory_space=pltpu.SMEM)


def anywhere():
    return pl.BlockSpec(memory_space=pl.ANY)


def cost(flops, moved, transcendentals=0):
    return pl.CostEstimate(flops=flops, bytes_accessed=moved, transcendentals=transcendentals)


def shaped(*shape, dtype=BF16):
    return jax.ShapeDtypeStruct(shape, dtype)


def local(kernel, outs, *args, scalars=0, moved=4 << 20, flops=0, limit=SMALL):
    return pl.pallas_call(
        kernel,
        in_specs=[smem()] * scalars + [vmem()] * (len(args) - scalars),
        out_specs=[vmem()] * len(outs),
        out_shape=outs,
        compiler_params=pltpu.CompilerParams(vmem_limit_bytes=limit),
        cost_estimate=cost(flops, moved),
    )(*args)


ORDER = (4, 6, 0, 3, 5, 2, 1)


def chunk_of(expert):
    return sum(((expert >> bit) & 1) << k for k, bit in enumerate(ORDER))


def send_kernel(
    experts, cap,
    ids_ref, weight_ref, scale_ref, codes_ref, grad_ref, gate, up, down,
    send_ref, row_ref, own_ref, table, place,
):
    step = pl.program_id(0)
    tokens, features = codes_ref.shape
    rows = send_ref.shape[0]

    @pl.when(step == 0)
    def _():
        ids = ids_ref[...]
        expert = iota((experts, tokens), 0)
        first, second = expert == ids[0:1, :], expert == ids[1:2, :]
        earlier = as_bf16(iota((tokens, tokens), 0) < iota((tokens, tokens), 1))
        count = dot(as_bf16(first | second), earlier)
        rank0 = jnp.sum(jnp.where(first, count, 0.0), axis=0, keepdims=True)
        rank1 = jnp.sum(jnp.where(second, count, 0.0), axis=0, keepdims=True)
        row0 = 2 * cap * chunk_of(ids[0:1, :]) + rank0.astype(I32)
        row1 = 2 * cap * chunk_of(ids[1:2, :]) + rank1.astype(I32)
        place[0:1, :] = row0
        place[1:2, :] = row1
        both = jnp.concatenate([row0.astype(F32), row1.astype(F32), jnp.zeros((tokens - 2, tokens), F32)], axis=0)
        row_ref[...] = both.T.astype(I32)
        blocks = scale_ref.shape[0]
        scale = jnp.concatenate([scale_ref[...], jnp.zeros((tokens - blocks, tokens), F32)], axis=0).T
        lanes = features // blocks
        for j in range(blocks):
            part = slice(j * lanes, (j + 1) * lanes)
            table[0:tokens, part] = (codes_ref[:, part].astype(F32) * scale[:, j : j + 1]).astype(BF16)
        table[tokens : 2 * tokens, :] = grad_ref[...]

    @pl.when(step == pl.num_programs(0) - 1)
    def _():
        own_ref[0] = gate[...]
        own_ref[1] = up[...]
        own_ref[2] = down[...].T

    row = iota((rows, tokens), 0) + step * rows
    is_grad = (row & cap) != 0
    base = row - (row & cap)
    in0, in1 = base == place[0:1, :], base == place[1:2, :]
    weight = jnp.sum(
        jnp.where(in0, weight_ref[0:1, :], 0.0) + jnp.where(in1, weight_ref[1:2, :], 0.0), axis=1, keepdims=True
    )
    weight = jnp.where(is_grad[:, 0:1], weight, 1.0)
    inside = in0 | in1
    pick = jnp.concatenate([as_bf16(inside & jnp.logical_not(is_grad)), as_bf16(inside & is_grad)], axis=1)
    width = 512
    for start in range(0, features, width):
        part = slice(start, start + width)
        send_ref[:, part] = (dot(pick, table[:, part]) * weight).astype(BF16)


def rows_to_send(ids, weights, scales, codes, grads, gate, up, down, experts, cap):
    tokens, features = codes.shape
    total = 2 * experts * cap
    rows = 512
    whole = lambda a: pl.BlockSpec(a.shape, lambda i: (0, 0))
    own = shaped(3, *gate.shape)
    args = (ids, weights, scales, codes, grads, gate, up, down)
    return pl.pallas_call(
        functools.partial(send_kernel, experts, cap),
        grid=(total // rows,),
        in_specs=[whole(a) for a in args],
        out_specs=[
            pl.BlockSpec((rows, features), lambda i: (i, 0)),
            pl.BlockSpec((tokens, tokens), lambda i: (0, 0)),
            pl.BlockSpec(own.shape, lambda i: (0, 0, 0)),
        ],
        out_shape=[shaped(total, features), shaped(tokens, tokens, dtype=I32), own],
        scratch_shapes=[pltpu.VMEM((2 * tokens, features), BF16), pltpu.VMEM((8, tokens), I32)],
        compiler_params=pltpu.CompilerParams(vmem_limit_bytes=VMEM),
        cost_estimate=cost(1 << 38, 6 << 20),
    )(*args)


def merge_kernel(own, chip, out):
    out[0] = own[...]
    out[1] = chip[...]


def arrange_kernel(dp_ref, mine, theirs, pre_mat, down_mat):
    width, hid = mine.shape[2:]
    for r, ref in enumerate((mine, theirs, mine, theirs)):
        at = pl.ds(pl.multiple_of((dp_ref[0] ^ r) * width, width), width)
        for k in range(2):
            pre_mat[at, k * hid : (k + 1) * hid] = ref[r // 2, k]
        down_mat[at, :] = ref[r // 2, 2]


def expert_weights(own, dp):
    width, hid = own.shape[1:]
    chip = lax.ppermute(own, "dp", OTHER_CHIP)
    (mine,) = local(merge_kernel, [shaped(2, 3, width, hid)], own, chip, flops=1 << 38)
    theirs = lax.ppermute(mine, "dp", OTHER_CORE)
    full = 4 * width
    return local(
        arrange_kernel,
        [shaped(full, 2 * hid), shaped(full, hid)],
        dp,
        mine,
        theirs,
        scalars=1,
        moved=12 << 20,
    )


def chunk_row(cap, rows, index):
    half = rows // 2
    slot = index & (half - 1)
    row = (slot // cap) * (2 * cap) + (slot & (cap - 1))
    return jnp.where(index >= half, row + cap, row)


def gather_matrix(cap, rows):
    return as_bf16(iota((rows, rows), 1) == chunk_row(cap, rows, iota((rows, rows), 0)))


def spread_matrix(cap, rows):
    return as_bf16(iota((rows, rows), 0) == chunk_row(cap, rows, iota((rows, rows), 1)))


def expert_kernel(
    cap,
    recv, pre_hbm, down_hbm,
    back_out, d_gu_out, hidden_out,
    landed, pre_mat, down_mat, x, dy, pre, d_hid, d_gu, hidden, dx, back,
    recv_sem, mat_sem, out_sem, back_sem,
):
    slots, features = x.shape
    hid = hidden.shape[1]
    blocks, block = landed.shape[:2]
    half = block // 2
    width = 512

    arrivals = [
        pltpu.make_async_copy(recv.at[pl.ds(b * block, block)], landed.at[b], recv_sem.at[b]) for b in range(blocks)
    ]
    mats = [
        pltpu.make_async_copy(src, dst, mat_sem.at[k])
        for k, (src, dst) in enumerate(((pre_hbm, pre_mat), (down_hbm, down_mat)))
    ]
    leaving = [
        pltpu.make_async_copy(src, dst, out_sem.at[k])
        for k, (src, dst) in enumerate(((d_gu, d_gu_out), (hidden, hidden_out)))
    ]
    returning = [
        pltpu.make_async_copy(back.at[b], back_out.at[pl.ds(b * block, block)], back_sem.at[b]) for b in range(blocks)
    ]
    for copy in arrivals + mats:
        copy.start()
    gather = gather_matrix(cap, block)
    for b in range(blocks):
        arrivals[b].wait()
        at = slice(b * half, (b + 1) * half)
        for start in range(0, features, width):
            part = slice(start, start + width)
            rows = dot(gather, landed[b, :, part]).astype(BF16)
            x[at, part] = rows[:half]
            dy[at, part] = rows[half:]
    mats[0].wait()
    wide = 256
    for m in range(0, slots, wide):
        pre[m : m + wide] = dot(x[m : m + wide], pre_mat[...])
    mats[1].wait()
    d_hid[...] = dot(dy[...], down_mat[...])

    step = 64

    @pl.loop(0, slots // step)
    def _(i):
        at = pl.ds(pl.multiple_of(i * step, step), step)
        pg, pu, dh = pre[at, 0:hid], pre[at, hid : 2 * hid], d_hid[at, :]
        sig = jax.nn.sigmoid(pg)
        act = pg * sig
        hidden[at, :] = (act * pu).astype(BF16)
        d_gu[at, 0:hid] = (dh * pu * sig * (1.0 + pg * (1.0 - sig))).astype(BF16)
        d_gu[at, hid : 2 * hid] = (dh * act).astype(BF16)

    for copy in leaving:
        copy.start()
    for start in range(0, features, width):
        part = slice(start, start + width)
        dx[:, part] = dot_turned(d_gu[...], pre_mat[part, :]).astype(BF16)
    spread = spread_matrix(cap, block)
    for b in range(blocks):
        at = slice(b * half, (b + 1) * half)
        for start in range(0, features // 2, width):
            low, high = slice(start, start + width), slice(features // 2 + start, features // 2 + start + width)
            rows = jnp.concatenate([dx[at, low], dx[at, high]], axis=0)
            back[b, :, low] = dot(spread, rows).astype(BF16)
        returning[b].start()
    for copy in leaving + returning:
        copy.wait()


def expert_rows(recv, pre_mat, down_mat, cap):
    total, features = recv.shape
    slots = total // 2
    hid = down_mat.shape[1]
    block = 256
    blocks = total // block
    outs = [(total, features // 2), (slots, 2 * hid), (slots, hid)]
    dma = pltpu.SemaphoreType.DMA
    return pl.pallas_call(
        functools.partial(expert_kernel, cap),
        in_specs=[anywhere()] * 3,
        out_specs=[anywhere()] * 3,
        out_shape=[shaped(*shape) for shape in outs],
        scratch_shapes=[
            pltpu.VMEM((blocks, block, features), BF16),
            pltpu.VMEM(pre_mat.shape, BF16),
            pltpu.VMEM(down_mat.shape, BF16),
            pltpu.VMEM((slots, features), BF16),
            pltpu.VMEM((slots, features), BF16),
            pltpu.VMEM((slots, 2 * hid), F32),
            pltpu.VMEM((slots, hid), F32),
            pltpu.VMEM((slots, 2 * hid), BF16),
            pltpu.VMEM((slots, hid), BF16),
            pltpu.VMEM((slots, features), BF16),
            pltpu.VMEM((blocks, block, features // 2), BF16),
            dma((blocks,)),
            dma((2,)),
            dma((2,)),
            dma((blocks,)),
        ],
        compiler_params=pltpu.CompilerParams(vmem_limit_bytes=VMEM),
        cost_estimate=cost(2 * slots * features * hid * 5, 16 << 20, slots * hid),
    )(recv, pre_mat, down_mat)


def odd_kernel(cap, dp_ref, recv, d_gu, hidden, out, turned_out, turned, x, dy):
    @pl.when(pl.program_id(0) == 0)
    def _():
        wide = d_gu.shape[1]
        turned[0:wide, :] = d_gu[...].T
        turned[wide:, :] = hidden[...].T
        turned_out[...] = turned[...]

    even_kernel(cap, dp_ref, recv, turned, out, x, dy)


def even_kernel(cap, dp_ref, recv, turned, out, x, dy):
    hid = out.shape[1]
    block = 256
    half = block // 2
    gather = gather_matrix(cap, block)
    for b in range(recv.shape[0] // block):
        rows = dot(gather, recv[b * block : (b + 1) * block, :]).astype(BF16)
        at = slice(b * half, (b + 1) * half)
        x[at, :] = rows[:half]
        dy[at, :] = rows[half:]
    for k, rows in enumerate((x, x, dy)):
        out[k] = dot(turned[k * hid : (k + 1) * hid, :], rows[...]).astype(BF16)


def partial_grads(kernel, first, dp, recv, grads, outs, scratch, cap):
    total, features = recv.shape
    width = features // 4
    whole = lambda a: pl.BlockSpec(a.shape, lambda i, dp: (0, 0))
    hid = outs[0].shape[2]
    return pl.pallas_call(
        functools.partial(kernel, cap),
        grid_spec=pltpu.PrefetchScalarGridSpec(
            num_scalar_prefetch=1,
            grid=(2,),
            in_specs=[pl.BlockSpec((total, width), lambda i, dp: (0, dp[0] ^ (2 * i + first)))] + [whole(g) for g in grads],
            out_specs=[pl.BlockSpec((None, 3, hid, width), lambda i, dp: (i, 0, 0, 0))] + [whole(o) for o in outs[1:]],
            scratch_shapes=scratch + [pltpu.VMEM((total // 2, width), BF16)] * 2,
        ),
        out_shape=outs,
        compiler_params=pltpu.CompilerParams(vmem_limit_bytes=VMEM),
        cost_estimate=cost(6 * total * width * hid, 6 << 20),
    )(dp, recv, *grads)


def first_kernel(even, given, down, gate_up, keep):
    for r in range(2):
        down[r] = add(even[r, 2], given[r, 2]).astype(BF16)
    for k in range(2):
        gate_up[k] = add(even[1, k], given[1, k]).astype(BF16)
        keep[k] = add(even[0, k], given[0, k]).astype(BF16)


def down_kernel(sent, other, out):
    out[0] = add(sent[0], other[1]).astype(BF16)
    out[1] = add(sent[1], other[0]).astype(BF16)


def gate_up_kernel(keep, other, gate, up):
    gate[...] = add(keep[0], other[0]).astype(BF16).T
    up[...] = add(keep[1], other[1]).astype(BF16).T


def place_kernel(dp_ref, even, odd, out):
    width = even.shape[2]
    for r, ref in enumerate((even, odd, even, odd)):
        out[:, pl.ds(pl.multiple_of((dp_ref[0] ^ r) * width, width), width)] = ref[r // 2]


def summed_grads(recv, d_gu, hidden, dp, grad_input, cap):
    features = recv.shape[1]
    slots, hid = hidden.shape
    width = features // 4
    part = shaped(2, 3, hid, width)
    turned = shaped(3 * hid, slots)
    odd, grads = partial_grads(
        odd_kernel, 1, dp, recv, (d_gu, hidden), [part, turned], [pltpu.VMEM(turned.shape, BF16)], cap
    )
    given = lax.ppermute(odd, "dp", OTHER_CORE)
    (even,) = partial_grads(even_kernel, 0, dp, recv, (grads,), [part], [], cap)
    two = shaped(2, hid, width)
    down, gate_up, keep = local(first_kernel, [two] * 3, even, given)
    down_other = lax.ppermute(down, "dp", OTHER_CHIP)
    gate_up_other = lax.ppermute(gate_up, "dp", OTHER_CHIP)
    (mine,) = local(down_kernel, [two], down, down_other)
    theirs = lax.ppermute(mine, "dp", OTHER_CORE)
    (grad_down,) = local(place_kernel, [shaped(hid, features)], dp, mine, theirs, scalars=1)
    grad_gate, grad_up = local(gate_up_kernel, [shaped(width, hid)] * 2, keep, gate_up_other)
    return grad_input, grad_gate, grad_up, grad_down


def token_kernel(cap, row_ref, recv_ref, out_ref):
    tokens, features = out_ref.shape
    total, half = recv_ref.shape
    row0, row1 = row_ref[:, 0:1], row_ref[:, 1:2]
    at = iota((tokens, total), 1)
    low = as_bf16((at == row0) | (at == row1))
    high = as_bf16((at == row0 + cap) | (at == row1 + cap))
    width = 512
    for p, pick in enumerate((low, high)):
        for start in range(0, half, width):
            value = dot(pick, recv_ref[:, start : start + width])
            out_ref[:, p * half + start : p * half + start + width] = value.astype(BF16)


def token_rows(row_of, recv, tokens, features, cap):
    return pl.pallas_call(
        functools.partial(token_kernel, cap),
        in_specs=[vmem(), vmem()],
        out_specs=vmem(),
        out_shape=shaped(tokens, features),
        compiler_params=pltpu.CompilerParams(vmem_limit_bytes=SMALL),
        cost_estimate=cost(4 * tokens * features * recv.shape[0], 3 << 20),
    )(row_of, recv)


def exchange(rows, experts):
    near = experts // 2
    order = sorted(range(experts), key=chunk_of)
    members = [
        [(2 * (chip ^ (e // near)) + core) * experts + e for e in order] for chip in range(2) for core in range(2)
    ]
    chunks = rows.reshape(experts, rows.shape[0] // experts, rows.shape[1])
    moved = lax.all_to_all(chunks, AXES, split_axis=0, concat_axis=0, axis_index_groups=members, tiled=True)
    return moved.reshape(rows.shape)


def per_device(codes, scales, grad_out, route_weight, expert_ids, w_gate, w_up, w_down):
    tokens, features = codes.shape
    experts = lax.axis_size("expert") * lax.axis_size("seq")
    cap = 2 * tokens * expert_ids.shape[1] // experts
    dp = lax.axis_index("dp").astype(I32).reshape(1)
    send, row_of, own = rows_to_send(
        expert_ids.T, route_weight.T, scales.T, codes, grad_out, w_gate[0], w_up[0], w_down[0], experts, cap
    )
    mats = expert_weights(own, dp)
    recv = exchange(send, experts)
    back, d_gu, hidden = expert_rows(recv, *mats, cap)
    returned = exchange(back, experts)
    grad_input = token_rows(row_of, returned, tokens, features, cap)
    grad_input, grad_gate, grad_up, grad_down = summed_grads(recv, d_gu, hidden, dp, grad_input, cap)
    return grad_input, grad_gate[None], grad_up[None], grad_down[None]


def solution(mesh):
    rows = P(AXES, None)
    split = P(("expert", "seq"), "dp", None)
    return jax.shard_map(
        per_device,
        mesh=mesh,
        in_specs=(rows, rows, rows, rows, rows, split, split, P(("expert", "seq"), None, "dp")),
        out_specs=(rows, split, split, P(("expert", "seq"), None, None)),
        check_vma=False,
    )
```

```python
import functools

import jax
import jax.numpy as jnp
from jax import lax
from jax.experimental import pallas as pl
from jax.experimental.pallas import tpu as pltpu
from jax.sharding import PartitionSpec as P

BF16 = jnp.bfloat16
F32 = jnp.float32
I32 = jnp.int32
VMEM = 56 << 20
SMALL = 24 << 20
AXES = ("dp", "expert", "seq")

OTHER_CORE = [(0, 1), (1, 0), (2, 3), (3, 2)]
OTHER_CHIP = [(0, 2), (2, 0), (1, 3), (3, 1)]


def iota(shape, dim):
    return lax.broadcasted_iota(I32, shape, dim)


def as_bf16(mask):
    return jnp.where(mask, 1.0, 0.0).astype(BF16)


def dot(a, b):
    return jnp.dot(a, b, preferred_element_type=F32)


def dot_turned(a, b):
    return lax.dot_general(a, b, (((1,), (1,)), ((), ())), preferred_element_type=F32)


def add(a, b):
    return a.astype(F32) + b.astype(F32)


def vmem():
    return pl.BlockSpec(memory_space=pltpu.VMEM)


def smem():
    return pl.BlockSpec(memory_space=pltpu.SMEM)


def anywhere():
    return pl.BlockSpec(memory_space=pl.ANY)


def cost(flops, moved, transcendentals=0):
    return pl.CostEstimate(flops=flops, bytes_accessed=moved, transcendentals=transcendentals)


def shaped(*shape, dtype=BF16):
    return jax.ShapeDtypeStruct(shape, dtype)


def local(kernel, outs, *args, scalars=0, moved=4 << 20, flops=0, limit=SMALL):
    return pl.pallas_call(
        kernel,
        in_specs=[smem()] * scalars + [vmem()] * (len(args) - scalars),
        out_specs=[vmem()] * len(outs),
        out_shape=outs,
        compiler_params=pltpu.CompilerParams(vmem_limit_bytes=limit),
        cost_estimate=cost(flops, moved),
    )(*args)


ORDER = (4, 6, 0, 3, 5, 2, 1)


def chunk_of(expert):
    return sum(((expert >> bit) & 1) << k for k, bit in enumerate(ORDER))


def send_kernel(
    experts, cap,
    ids_ref, weight_ref, scale_ref, codes_ref, grad_ref, gate, up, down,
    send_ref, row_ref, own_ref, table, place,
):
    step = pl.program_id(0)
    tokens, features = codes_ref.shape
    rows = send_ref.shape[0]

    @pl.when(step == 0)
    def _():
        ids = ids_ref[...]
        expert = iota((experts, tokens), 0)
        first, second = expert == ids[0:1, :], expert == ids[1:2, :]
        earlier = as_bf16(iota((tokens, tokens), 0) < iota((tokens, tokens), 1))
        count = dot(as_bf16(first | second), earlier)
        rank0 = jnp.sum(jnp.where(first, count, 0.0), axis=0, keepdims=True)
        rank1 = jnp.sum(jnp.where(second, count, 0.0), axis=0, keepdims=True)
        row0 = 2 * cap * chunk_of(ids[0:1, :]) + rank0.astype(I32)
        row1 = 2 * cap * chunk_of(ids[1:2, :]) + rank1.astype(I32)
        place[0:1, :] = row0
        place[1:2, :] = row1
        both = jnp.concatenate([row0.astype(F32), row1.astype(F32), jnp.zeros((tokens - 2, tokens), F32)], axis=0)
        row_ref[...] = both.T.astype(I32)
        blocks = scale_ref.shape[0]
        scale = jnp.concatenate([scale_ref[...], jnp.zeros((tokens - blocks, tokens), F32)], axis=0).T
        lanes = features // blocks
        for j in range(blocks):
            part = slice(j * lanes, (j + 1) * lanes)
            table[0:tokens, part] = (codes_ref[:, part].astype(F32) * scale[:, j : j + 1]).astype(BF16)
        table[tokens : 2 * tokens, :] = grad_ref[...]

    @pl.when(step == pl.num_programs(0) - 1)
    def _():
        own_ref[0] = gate[...]
        own_ref[1] = up[...]
        own_ref[2] = down[...].T

    row = iota((rows, tokens), 0) + step * rows
    is_grad = (row & cap) != 0
    base = row - (row & cap)
    in0, in1 = base == place[0:1, :], base == place[1:2, :]
    weight = jnp.sum(
        jnp.where(in0, weight_ref[0:1, :], 0.0) + jnp.where(in1, weight_ref[1:2, :], 0.0), axis=1, keepdims=True
    )
    weight = jnp.where(is_grad[:, 0:1], weight, 1.0)
    inside = in0 | in1
    pick = jnp.concatenate([as_bf16(inside & jnp.logical_not(is_grad)), as_bf16(inside & is_grad)], axis=1)
    width = 512
    for start in range(0, features, width):
        part = slice(start, start + width)
        send_ref[:, part] = (dot(pick, table[:, part]) * weight).astype(BF16)


def rows_to_send(ids, weights, scales, codes, grads, gate, up, down, experts, cap):
    tokens, features = codes.shape
    total = 2 * experts * cap
    rows = 512
    whole = lambda a: pl.BlockSpec(a.shape, lambda i: (0, 0))
    own = shaped(3, *gate.shape)
    args = (ids, weights, scales, codes, grads, gate, up, down)
    return pl.pallas_call(
        functools.partial(send_kernel, experts, cap),
        grid=(total // rows,),
        in_specs=[whole(a) for a in args],
        out_specs=[
            pl.BlockSpec((rows, features), lambda i: (i, 0)),
            pl.BlockSpec((tokens, tokens), lambda i: (0, 0)),
            pl.BlockSpec(own.shape, lambda i: (0, 0, 0)),
        ],
        out_shape=[shaped(total, features), shaped(tokens, tokens, dtype=I32), own],
        scratch_shapes=[pltpu.VMEM((2 * tokens, features), BF16), pltpu.VMEM((8, tokens), I32)],
        compiler_params=pltpu.CompilerParams(vmem_limit_bytes=VMEM),
        cost_estimate=cost(1 << 38, 6 << 20),
    )(*args)


def merge_kernel(own, chip, out):
    out[0] = own[...]
    out[1] = chip[...]


def arrange_kernel(dp_ref, mine, theirs, pre_mat, down_mat):
    width, hid = mine.shape[2:]
    for r, ref in enumerate((mine, theirs, mine, theirs)):
        at = pl.ds(pl.multiple_of((dp_ref[0] ^ r) * width, width), width)
        for k in range(2):
            pre_mat[at, k * hid : (k + 1) * hid] = ref[r // 2, k]
        down_mat[at, :] = ref[r // 2, 2]


def expert_weights(own, dp):
    width, hid = own.shape[1:]
    chip = lax.ppermute(own, "dp", OTHER_CHIP)
    (mine,) = local(merge_kernel, [shaped(2, 3, width, hid)], own, chip, flops=1 << 38)
    theirs = lax.ppermute(mine, "dp", OTHER_CORE)
    full = 4 * width
    return local(
        arrange_kernel,
        [shaped(full, 2 * hid), shaped(full, hid)],
        dp,
        mine,
        theirs,
        scalars=1,
        moved=12 << 20,
    )


def chunk_row(cap, rows, index):
    half = rows // 2
    slot = index & (half - 1)
    row = (slot // cap) * (2 * cap) + (slot & (cap - 1))
    return jnp.where(index >= half, row + cap, row)


def gather_matrix(cap, rows):
    return as_bf16(iota((rows, rows), 1) == chunk_row(cap, rows, iota((rows, rows), 0)))


def spread_matrix(cap, rows):
    return as_bf16(iota((rows, rows), 0) == chunk_row(cap, rows, iota((rows, rows), 1)))


def expert_kernel(
    cap,
    recv, pre_hbm, down_hbm,
    back_out, d_gu_out, hidden_out,
    landed, pre_mat, down_mat, x, dy, pre, d_hid, d_gu, hidden, dx, back,
    recv_sem, mat_sem, out_sem, back_sem,
):
    slots, features = x.shape
    hid = hidden.shape[1]
    blocks, block = landed.shape[:2]
    half = block // 2
    width = 512

    arrivals = [
        pltpu.make_async_copy(recv.at[pl.ds(b * block, block)], landed.at[b], recv_sem.at[b]) for b in range(blocks)
    ]
    mats = [
        pltpu.make_async_copy(src, dst, mat_sem.at[k])
        for k, (src, dst) in enumerate(((pre_hbm, pre_mat), (down_hbm, down_mat)))
    ]
    leaving = [
        pltpu.make_async_copy(src, dst, out_sem.at[k])
        for k, (src, dst) in enumerate(((d_gu, d_gu_out), (hidden, hidden_out)))
    ]
    returning = [
        pltpu.make_async_copy(back.at[b], back_out.at[pl.ds(b * block, block)], back_sem.at[b]) for b in range(blocks)
    ]
    for copy in arrivals + mats[::-1]:
        copy.start()
    gather = gather_matrix(cap, block)
    for b in range(blocks):
        arrivals[b].wait()
        at = slice(b * half, (b + 1) * half)
        for start in range(0, features, width):
            part = slice(start, start + width)
            rows = dot(gather, landed[b, :, part]).astype(BF16)
            x[at, part] = rows[:half]
            dy[at, part] = rows[half:]
    mats[1].wait()
    d_hid[...] = dot(dy[...], down_mat[...])
    mats[0].wait()
    wide = 256
    for m in range(0, slots, wide):
        pre[m : m + wide] = dot(x[m : m + wide], pre_mat[...])

    step = 64

    @pl.loop(0, slots // step)
    def _(i):
        at = pl.ds(pl.multiple_of(i * step, step), step)
        pg, pu, dh = pre[at, 0:hid], pre[at, hid : 2 * hid], d_hid[at, :]
        sig = jax.nn.sigmoid(pg)
        act = pg * sig
        hidden[at, :] = (act * pu).astype(BF16)
        d_gu[at, 0:hid] = (dh * pu * sig * (1.0 + pg * (1.0 - sig))).astype(BF16)
        d_gu[at, hid : 2 * hid] = (dh * act).astype(BF16)

    for copy in leaving:
        copy.start()
    for start in range(0, features, width):
        part = slice(start, start + width)
        dx[:, part] = dot_turned(d_gu[...], pre_mat[part, :]).astype(BF16)
    spread = spread_matrix(cap, block)
    for b in range(blocks):
        at = slice(b * half, (b + 1) * half)
        for start in range(0, features // 2, width):
            low, high = slice(start, start + width), slice(features // 2 + start, features // 2 + start + width)
            rows = jnp.concatenate([dx[at, low], dx[at, high]], axis=0)
            back[b, :, low] = dot(spread, rows).astype(BF16)
        returning[b].start()
    for copy in leaving + returning:
        copy.wait()


def expert_rows(recv, pre_mat, down_mat, cap):
    total, features = recv.shape
    slots = total // 2
    hid = down_mat.shape[1]
    block = 256
    blocks = total // block
    outs = [(total, features // 2), (slots, 2 * hid), (slots, hid)]
    dma = pltpu.SemaphoreType.DMA
    return pl.pallas_call(
        functools.partial(expert_kernel, cap),
        in_specs=[anywhere()] * 3,
        out_specs=[anywhere()] * 3,
        out_shape=[shaped(*shape) for shape in outs],
        scratch_shapes=[
            pltpu.VMEM((blocks, block, features), BF16),
            pltpu.VMEM(pre_mat.shape, BF16),
            pltpu.VMEM(down_mat.shape, BF16),
            pltpu.VMEM((slots, features), BF16),
            pltpu.VMEM((slots, features), BF16),
            pltpu.VMEM((slots, 2 * hid), F32),
            pltpu.VMEM((slots, hid), F32),
            pltpu.VMEM((slots, 2 * hid), BF16),
            pltpu.VMEM((slots, hid), BF16),
            pltpu.VMEM((slots, features), BF16),
            pltpu.VMEM((blocks, block, features // 2), BF16),
            dma((blocks,)),
            dma((2,)),
            dma((2,)),
            dma((blocks,)),
        ],
        compiler_params=pltpu.CompilerParams(vmem_limit_bytes=VMEM),
        cost_estimate=cost(2 * slots * features * hid * 5, 16 << 20, slots * hid),
    )(recv, pre_mat, down_mat)


def odd_kernel(cap, dp_ref, recv, d_gu, hidden, out, turned_out, turned, x, dy):
    @pl.when(pl.program_id(0) == 0)
    def _():
        wide = d_gu.shape[1]
        turned[0:wide, :] = d_gu[...].T
        turned[wide:, :] = hidden[...].T
        turned_out[...] = turned[...]

    even_kernel(cap, dp_ref, recv, turned, out, x, dy)


def even_kernel(cap, dp_ref, recv, turned, out, x, dy):
    hid = out.shape[1]
    block = 256
    half = block // 2
    gather = gather_matrix(cap, block)
    for b in range(recv.shape[0] // block):
        rows = dot(gather, recv[b * block : (b + 1) * block, :]).astype(BF16)
        at = slice(b * half, (b + 1) * half)
        x[at, :] = rows[:half]
        dy[at, :] = rows[half:]
    for k, rows in enumerate((x, x, dy)):
        out[k] = dot(turned[k * hid : (k + 1) * hid, :], rows[...]).astype(BF16)


def partial_grads(kernel, first, dp, recv, grads, outs, scratch, cap):
    total, features = recv.shape
    width = features // 4
    whole = lambda a: pl.BlockSpec(a.shape, lambda i, dp: (0, 0))
    hid = outs[0].shape[2]
    return pl.pallas_call(
        functools.partial(kernel, cap),
        grid_spec=pltpu.PrefetchScalarGridSpec(
            num_scalar_prefetch=1,
            grid=(2,),
            in_specs=[pl.BlockSpec((total, width), lambda i, dp: (0, dp[0] ^ (2 * i + first)))] + [whole(g) for g in grads],
            out_specs=[pl.BlockSpec((None, 3, hid, width), lambda i, dp: (i, 0, 0, 0))] + [whole(o) for o in outs[1:]],
            scratch_shapes=scratch + [pltpu.VMEM((total // 2, width), BF16)] * 2,
        ),
        out_shape=outs,
        compiler_params=pltpu.CompilerParams(vmem_limit_bytes=VMEM),
        cost_estimate=cost(6 * total * width * hid, 6 << 20),
    )(dp, recv, *grads)


def first_kernel(even, given, down, gate_up, keep):
    for r in range(2):
        down[r] = add(even[r, 2], given[r, 2]).astype(BF16)
    for k in range(2):
        gate_up[k] = add(even[1, k], given[1, k]).astype(BF16)
        keep[k] = add(even[0, k], given[0, k]).astype(BF16)


def down_kernel(sent, other, out):
    out[0] = add(sent[0], other[1]).astype(BF16)
    out[1] = add(sent[1], other[0]).astype(BF16)


def gate_up_kernel(keep, other, gate, up):
    gate[...] = add(keep[0], other[0]).astype(BF16).T
    up[...] = add(keep[1], other[1]).astype(BF16).T


def place_kernel(dp_ref, even, odd, out):
    width = even.shape[2]
    for r, ref in enumerate((even, odd, even, odd)):
        out[:, pl.ds(pl.multiple_of((dp_ref[0] ^ r) * width, width), width)] = ref[r // 2]


def summed_grads(recv, d_gu, hidden, dp, grad_input, cap):
    features = recv.shape[1]
    slots, hid = hidden.shape
    width = features // 4
    part = shaped(2, 3, hid, width)
    turned = shaped(3 * hid, slots)
    odd, grads = partial_grads(
        odd_kernel, 1, dp, recv, (d_gu, hidden), [part, turned], [pltpu.VMEM(turned.shape, BF16)], cap
    )
    given = lax.ppermute(odd, "dp", OTHER_CORE)
    (even,) = partial_grads(even_kernel, 0, dp, recv, (grads,), [part], [], cap)
    two = shaped(2, hid, width)
    down, gate_up, keep = local(first_kernel, [two] * 3, even, given)
    down_other = lax.ppermute(down, "dp", OTHER_CHIP)
    gate_up_other = lax.ppermute(gate_up, "dp", OTHER_CHIP)
    (mine,) = local(down_kernel, [two], down, down_other)
    theirs = lax.ppermute(mine, "dp", OTHER_CORE)
    (grad_down,) = local(place_kernel, [shaped(hid, features)], dp, mine, theirs, scalars=1)
    grad_gate, grad_up = local(gate_up_kernel, [shaped(width, hid)] * 2, keep, gate_up_other)
    return grad_input, grad_gate, grad_up, grad_down


def token_kernel(cap, row_ref, recv_ref, out_ref):
    tokens, features = out_ref.shape
    total, half = recv_ref.shape
    row0, row1 = row_ref[:, 0:1], row_ref[:, 1:2]
    at = iota((tokens, total), 1)
    low = as_bf16((at == row0) | (at == row1))
    high = as_bf16((at == row0 + cap) | (at == row1 + cap))
    width = 512
    for p, pick in enumerate((low, high)):
        for start in range(0, half, width):
            value = dot(pick, recv_ref[:, start : start + width])
            out_ref[:, p * half + start : p * half + start + width] = value.astype(BF16)


def token_rows(row_of, recv, tokens, features, cap):
    return pl.pallas_call(
        functools.partial(token_kernel, cap),
        in_specs=[vmem(), vmem()],
        out_specs=vmem(),
        out_shape=shaped(tokens, features),
        compiler_params=pltpu.CompilerParams(vmem_limit_bytes=SMALL),
        cost_estimate=cost(4 * tokens * features * recv.shape[0], 3 << 20),
    )(row_of, recv)


def exchange(rows, experts):
    near = experts // 2
    order = sorted(range(experts), key=chunk_of)
    members = [
        [(2 * (chip ^ (e // near)) + core) * experts + e for e in order] for chip in range(2) for core in range(2)
    ]
    chunks = rows.reshape(experts, rows.shape[0] // experts, rows.shape[1])
    moved = lax.all_to_all(chunks, AXES, split_axis=0, concat_axis=0, axis_index_groups=members, tiled=True)
    return moved.reshape(rows.shape)


def per_device(codes, scales, grad_out, route_weight, expert_ids, w_gate, w_up, w_down):
    tokens, features = codes.shape
    experts = lax.axis_size("expert") * lax.axis_size("seq")
    cap = 2 * tokens * expert_ids.shape[1] // experts
    dp = lax.axis_index("dp").astype(I32).reshape(1)
    send, row_of, own = rows_to_send(
        expert_ids.T, route_weight.T, scales.T, codes, grad_out, w_gate[0], w_up[0], w_down[0], experts, cap
    )
    mats = expert_weights(own, dp)
    recv = exchange(send, experts)
    back, d_gu, hidden = expert_rows(recv, *mats, cap)
    returned = exchange(back, experts)
    grad_input = token_rows(row_of, returned, tokens, features, cap)
    grad_input, grad_gate, grad_up, grad_down = summed_grads(recv, d_gu, hidden, dp, grad_input, cap)
    return grad_input, grad_gate[None], grad_up[None], grad_down[None]


def solution(mesh):
    rows = P(AXES, None)
    split = P(("expert", "seq"), "dp", None)
    return jax.shard_map(
        per_device,
        mesh=mesh,
        in_specs=(rows, rows, rows, rows, rows, split, split, P(("expert", "seq"), None, "dp")),
        out_specs=(rows, split, split, P(("expert", "seq"), None, None)),
        check_vma=False,
    )
```
